32 devices in a mesh: dp: 4 (over y, core), expert: 8 (over z, x).
Axes of the slice: x: 2, y: 2, z: 4, core: 2. Of those that a mesh axis runs over, the one named last changes fastest.
Arguments:
- grad_out: bfloat16 [4096, 2048], P(('dp', 'expert')), may hold values from -6 to 6
- route_prob: bfloat16 [4096, 1], P(('dp', 'expert')), may hold values from 0.099609375 to 1
- expert_ids: int32 [4096, 1], P(('dp', 'expert')), may hold values from 0 to 7; in each aligned block of 128 rows (0 to 127, 128 to 255, ...) at most 24 rows name the same one
- saved_act: bfloat16 [4, 8, 192, 768], P('dp', 'expert'), may hold values from -0.21875 to 0.21875
- down_weight: bfloat16 [8, 768, 2048], P('expert'), may hold values from -0.21875 to 0.21875
Outputs:
- grad_act: bfloat16 [4, 8, 192, 768], P('dp', 'expert')
- grad_weight: float32 [8, 2048, 768], P('expert', 'dp')
- grad_prob: float32 [4096, 1], P(('dp', 'expert'))
The draws below stay inside these ranges and needn't reach their ends.
Inputs may be any that keep to these rules, and one draw needn't show every extreme that they name: `expert_ids`: among the 128 tokens of one device no expert is named more than 24 times, a bound that some block reaches on every device.
All inputs are finite; a program needn't handle non-finite values.
Results may differ from the reference program's by a relative error of at most 0.0029.
Values may be sent and summed in bfloat16 or wider, within the bound.
No kernel may reach another device: no remote copies, remote signals or barrier semaphores. Data moves between devices by JAX's collectives and lax.ppermute only.
A program may use at most 64 MiB of HBM per device.

```python
import math
import jax
import jax.numpy as jnp
import numpy as np
from jax import lax

D = 2048
FFW = 768
ROUTED = 1
TOK_DEV = 128
EXPERTS = 8
CAP = 24
SLOTS = 192
TOKENS = 4096
N_DP = 4
N_EXPERT = 8


def steps_of(stream_key, shape, cuts, smallest, top_value):
    def one(axis_at, parts):
        heights = jax.random.uniform(jax.random.fold_in(jax.random.fold_in(stream_key, 6), axis_at), (parts,), jnp.float32, smallest / len(cuts), top_value / len(cuts))
        return jnp.repeat(jnp.exp(heights), shape[axis_at] // parts).reshape((-1,) + (1,) * (len(shape) - axis_at - 1))

    factor_of = one(*cuts[0])
    for cut in cuts[1:]:
        factor_of = factor_of * one(*cut)
    return factor_of


def routed_block(stream_key, own, number, rows, number_of, top, reach, skew):
    order = jax.random.permutation(stream_key, number_of)
    packed, ordinary = shares(number_of, rows * top, reach, skew, True), shares(number_of, rows * top, reach, skew, False)
    places = jnp.arange(number_of)

    def named(sizes, turn):
        used = int((sizes > 0).sum())
        fixed = max(1, used // 4)
        passed = fixed + (places - fixed + turn * (used - fixed)) % max(1, number_of - fixed)
        return jnp.zeros((number_of,), jnp.int32).at[order[jnp.where(places < fixed, places, passed)]].set(jnp.asarray(sizes, jnp.int32))

    sizes = jnp.where(number % 4 == 0, named(packed, number // 4), named(ordinary, number - number // 4 - 1))
    mixed = jax.random.permutation(jax.random.fold_in(own, 3), number_of)
    source_of, receiver = mixed[0:number_of // 2 * 2:2], mixed[1:number_of // 2 * 2:2]
    slack = jnp.minimum(sizes[source_of] - 1, reach - sizes[receiver]) // 2
    slack = jnp.where((source_of == order[0]) | (receiver == order[0]) | (sizes[receiver] == 0), 0, jnp.maximum(slack, 0))
    passed = jax.random.randint(jax.random.fold_in(own, 4), (number_of // 2,), 0, 1 << 20) % (slack + 1)
    sizes = sizes.at[source_of].add(-passed).at[receiver].add(passed)
    members = jnp.searchsorted(jnp.cumsum(sizes), jnp.arange(rows * top), side="right").astype(jnp.int32)
    grid = members.reshape(top, rows).T
    grid = grid[jax.random.permutation(jax.random.fold_in(own, 1), rows)]
    turn = jax.random.randint(jax.random.fold_in(own, 2), (rows, 1), 0, top)
    return jnp.take_along_axis(grid, (jnp.arange(top)[None, :] + turn) % top, axis=1)


def shares(count, total, limit, skew, full):
    portions = [(1 << 20) // math.isqrt(standing ** skew) + 1 for standing in range(1, count + 1)]
    largest = limit if full else min(limit, max(-(-total // count), total * portions[0] // sum(portions)))
    least = 1 if total - largest >= count - 1 else 0
    counts, surplus = [largest] + [least] * (count - 1), total - largest - least * (count - 1)
    while surplus > 0:
        movable = [i for i in range(1, count) if counts[i] < largest] or [i for i in range(1, count) if counts[i] < limit]
        whole, budget = sum([portions[i] for i in movable]), surplus
        for i in movable:
            extra = min(limit - counts[i], max(1, budget * portions[i] // whole), surplus)
            counts[i] = counts[i] + extra
            surplus = surplus - extra
    return np.array(counts)


def noise(rng, shape, width, reach, shards=(), kind=jnp.bfloat16):
    result = jax.random.normal(rng, shape, jnp.float32) * width
    if len(shards) > 0:
        result = steps_of(rng, shape, shards, -0.22, 0.18) * result
    return jnp.clip(result, min=-reach, max=reach).astype(kind)


def setup_inputs(seed: int = 0) -> dict:
    streams_of = jax.random.split(jax.random.key(seed), 6)
    grad_out = noise(streams_of[0], (TOKENS, D), 1.0, 6.0, ((0, 32),))
    route_prob = jnp.clip(0.099609375 + 0.9003906 * jax.random.uniform(streams_of[1], (TOKENS, ROUTED), jnp.float32) ** steps_of(streams_of[1], (TOKENS, ROUTED), ((0, 32),), -0.2, 0.2), 0.099609375, 1.0).astype(jnp.bfloat16)
    expert_ids_keys = jax.random.split(jax.random.fold_in(streams_of[2], 1), TOKENS // TOK_DEV)
    expert_ids_turns = jax.random.permutation(jax.random.fold_in(streams_of[2], 3), TOKENS // TOK_DEV)
    expert_ids = jax.vmap(lambda own, number: routed_block(jax.random.fold_in(streams_of[2], 2), own, number, TOK_DEV, EXPERTS, 1, CAP, 2))(expert_ids_keys, expert_ids_turns).reshape((TOKENS, ROUTED))
    saved_act = noise(streams_of[3], (N_DP, EXPERTS, SLOTS, FFW), (FFW ** -0.5), 0.21875, ((0, 4), (1, 8)))
    down_weight = noise(streams_of[4], (EXPERTS, FFW, D), FFW ** -0.5, 0.21875, ((0, 8),))
    return {"grad_out": grad_out, "route_prob": route_prob, "expert_ids": expert_ids, "saved_act": saved_act, "down_weight": down_weight}


def reference(grad_out, route_prob, expert_ids, saved_act, down_weight):
    groups = N_DP * N_EXPERT
    routed = expert_ids[:, 0].reshape(groups, TOK_DEV)
    member = (routed[:, :, None] == jnp.arange(EXPERTS, dtype=jnp.int32)[None, None, :]).astype(jnp.int32)
    before = jnp.cumsum(member, axis=1) - member
    within = jnp.sum(before * member, axis=2)
    device = jnp.arange(groups, dtype=jnp.int32)[:, None]
    source = device % N_EXPERT
    replica = device // N_EXPERT
    position = source * CAP + within
    flat_index = ((replica * EXPERTS + routed) * SLOTS + position).reshape(-1).astype(jnp.int32)
    token_index = jnp.arange(TOKENS, dtype=jnp.int32)
    lookup = jnp.full((N_DP * EXPERTS * SLOTS,), TOKENS, jnp.int32).at[flat_index].set(token_index)
    lookup = lookup.reshape(N_DP, EXPERTS, SLOTS)
    prob_column = route_prob[:, 0]

    def one_expert(expert):
        chosen = lookup[:, expert]
        arrived = jnp.take(grad_out, chosen, axis=0, mode="fill", fill_value=0).astype(jnp.float32)
        arrived_prob = jnp.take(prob_column, chosen, axis=0, mode="fill", fill_value=0).astype(jnp.float32)[..., None]
        stored = saved_act[:, expert].astype(jnp.float32)
        weight = down_weight[expert].astype(jnp.float32)
        backed = jnp.einsum("rsd,fd->rsf", arrived, weight)
        grad_act = (arrived_prob * backed).astype(jnp.bfloat16)
        slot_grad = jnp.sum(backed * stored, axis=2)
        weighted = lax.optimization_barrier((arrived_prob * arrived).astype(jnp.bfloat16)).astype(jnp.float32)
        partial_value = jnp.einsum("rsd,rsf->rdf", weighted, stored)
        return grad_act, jnp.sum(partial_value, axis=0), slot_grad

    grad_act, grad_weight, slot_grad = lax.map(one_expert, jnp.arange(EXPERTS, dtype=jnp.int32))
    grad_act = jnp.transpose(grad_act, (1, 0, 2, 3))
    slot_flat = jnp.transpose(slot_grad, (1, 0, 2)).reshape(-1)
    grad_prob = slot_flat[flat_index][:, None]
    return grad_act, grad_weight, grad_prob
```

```python
import functools

import jax
import jax.numpy as jnp
from jax import lax
from jax.experimental import pallas as pl
from jax.experimental.pallas import tpu as pltpu
from jax.sharding import PartitionSpec as P

LANES = 128
F32 = jnp.float32
BF16 = jnp.bfloat16
ORDER = (4, 1, 5, 2, 6, 7, 3, 0)
LATE = 6


def kernel_call(body, outs, operands, name, flops=0, scratch=(), stay=()):
    nbytes = sum(a.size * a.dtype.itemsize for a in (*outs, *operands))
    vmem, hbm = pl.BlockSpec(memory_space=pltpu.VMEM), pl.BlockSpec(memory_space=pltpu.HBM)
    operands = [
        pltpu.with_memory_space_constraint(a, pltpu.HBM) if i in stay else a
        for i, a in enumerate(operands)
    ]
    return pl.pallas_call(
        body,
        out_shape=outs,
        in_specs=[hbm if i in stay else vmem for i in range(len(operands))],
        out_specs=[vmem] * len(outs),
        scratch_shapes=scratch,
        compiler_params=pltpu.CompilerParams(vmem_limit_bytes=16 * 2**20),
        cost_estimate=pl.CostEstimate(flops=flops, bytes_accessed=nbytes, transcendentals=0),
        name=name,
    )(*operands)


def shape(dims, kind):
    return jax.ShapeDtypeStruct(dims, kind)


def dot(a, b, dims=((1,), (0,)), precision=None):
    return lax.dot_general(
        a, b, (dims, ((), ())), preferred_element_type=F32, precision=precision
    )


def iota(dims, axis):
    return lax.broadcasted_iota(jnp.int32, dims, axis)


def place_body(experts, order, cap, *refs):
    (ids_hbm, prob_hbm, rows_hbm), refs = refs[:3], refs[3:]
    *chunk_refs, within_ref, ids_ref, prob_ref, rows_ref, sems = refs
    copies = [
        pltpu.make_async_copy(source, target, sems.at[i])
        for i, (source, target) in enumerate(
            ((ids_hbm, ids_ref), (prob_hbm, prob_ref), (rows_hbm, rows_ref))
        )
    ]
    for copy in copies:
        copy.start()
    tokens, width = rows_ref.shape
    copies[0].wait()
    ids = ids_ref[...]
    slots, rows = experts * cap, chunk_refs[0].shape[0]
    member = (iota((experts, tokens), 0) == ids).astype(F32)
    earlier = (iota((tokens, tokens), 0) < iota((tokens, tokens), 1)).astype(BF16)
    before = dot(member.astype(BF16), earlier)
    within = jnp.sum(before * member, axis=0, keepdims=True).astype(jnp.int32)
    within_ref[...] = within
    partner = ids ^ lax.axis_index("expert")
    place = 0
    for i, k in enumerate(order):
        place = jnp.where(partner == k, i, place)
    if not order:
        place = ids
    chosen = iota((slots, tokens), 0) == place * cap + within
    copies[1].wait()
    prob = jnp.sum(jnp.where(chosen, prob_ref[...].astype(F32), 0.0), axis=1, keepdims=True)
    chosen = chosen.astype(BF16)
    copies[2].wait()

    def put(columns, values):
        for i, ref in enumerate(chunk_refs):
            ref[:, columns] = values[i * rows : (i + 1) * rows].astype(BF16)

    step = 2 * LANES
    for c in range(0, width, step):
        put(slice(c, c + step), dot(chosen, rows_ref[:, c : c + step]))
    put(slice(width, width + LANES), jnp.broadcast_to(prob, (slots, LANES)))


def weigh_body(replicas, order, *refs):
    n_dp = len(replicas)
    *chunk_refs, rows_ref, prob_ref = refs[: -n_dp - 1]
    weighted_refs, all_ref = refs[-n_dp - 1 : -1], refs[-1]
    width = rows_ref.shape[1]
    chunk = width // n_dp
    size = chunk_refs[0].shape[0]
    for c in range(0, width + LANES, LANES):
        columns = slice(c, c + LANES)
        for k, ref in zip(order or (0,), chunk_refs):
            at = (lax.axis_index("expert") ^ k) * size if order else 0
            all_ref[pl.ds(at, size), columns] = ref[:, columns].astype(F32)
    prob = all_ref[:, width:]
    prob_ref[...] = prob
    replica = lax.axis_index("dp")
    for k, ref in zip(replicas, weighted_refs):
        for c in range(0, chunk, LANES):
            columns = pl.ds(pl.multiple_of((replica ^ k) * chunk + c, LANES), LANES)
            piece = all_ref[:, columns]
            rows_ref[:, columns] = piece.astype(BF16)
            ref[:, c : c + LANES] = (piece * prob).astype(BF16)


def fetch_body(weight_hbm, out_ref, sem):
    copy = pltpu.make_async_copy(weight_hbm, out_ref, sem)
    copy.start()
    copy.wait()


def by_source(column, experts, cap):
    slots = experts * cap
    spread = jnp.where(iota((slots, LANES), 1) == iota((slots, LANES), 0) % cap, column, 0.0)
    if cap % 8 == 0:
        return jnp.sum(spread.reshape(experts, cap, LANES), axis=1)
    owner = (iota((experts, slots), 0) == iota((experts, slots), 1) // cap).astype(F32)
    return dot(owner, spread, precision=lax.Precision.HIGHEST)


def act_body(experts, cap, rows_ref, prob_ref, weight_ref, stored_ref, act_ref, table_ref):
    backed = dot(rows_ref[...], weight_ref[...], ((1,), (1,)))
    act_ref[...] = (prob_ref[:, 0:1] * backed).astype(BF16)
    column = jnp.sum(backed * stored_ref[...].astype(F32), axis=1, keepdims=True)
    table = by_source(column, experts, cap)
    table_ref[...] = jnp.broadcast_to(table[:, None], table_ref.shape)


def gradient_body(n_dp, *refs):
    lhs = jnp.concatenate([ref[...] for ref in refs[:n_dp]], axis=0)
    rhs = jnp.concatenate([ref[...] for ref in refs[n_dp:-1]], axis=0)
    refs[-1][...] = dot(lhs, rhs, ((0,), (0,)))


def pick_body(experts, ids_ref, within_ref, table_ref, out_ref):
    ids = ids_ref[...]
    tokens = ids.shape[1]
    at = jnp.broadcast_to(within_ref[...], (experts, tokens))
    values = jnp.take_along_axis(table_ref[:, 0, :], at, axis=1, mode="promise_in_bounds")
    member = iota((experts, tokens), 0) == ids
    out_ref[...] = jnp.sum(jnp.where(member, values, 0.0), axis=0, keepdims=True)


def shards(n_dp, experts, grad_out, route_prob, expert_ids, saved_act, down_weight):
    slots, ffw = saved_act.shape[2:]
    cap = slots // experts
    tokens, width = grad_out.shape
    chunk = width // n_dp
    stored = saved_act[0, 0]
    order = ORDER if experts == len(ORDER) else ()
    chunks = max(len(order), 1)
    ids = expert_ids.reshape(1, tokens)
    prob_row = route_prob.reshape(1, tokens)

    def swap(array, axis, k):
        size = lax.axis_size(axis)
        return lax.ppermute(array, axis, [(r, r ^ k) for r in range(size)])

    def exchange(array):
        return lax.all_to_all(array, "expert", split_axis=0, concat_axis=0, tiled=True)

    *packed, within = kernel_call(
        functools.partial(place_body, experts, order, cap),
        (shape((slots // chunks, width + LANES), BF16),) * chunks + (shape((1, tokens), jnp.int32),),
        (ids, prob_row, grad_out),
        flops=2 * slots * tokens * width,
        name="place",
        stay=(0, 1, 2),
        scratch=(
            pltpu.VMEM((1, tokens), jnp.int32),
            pltpu.VMEM((1, tokens), BF16),
            pltpu.VMEM((tokens, width), BF16),
            pltpu.SemaphoreType.DMA((3,)),
        ),
    )
    (weight,) = kernel_call(
        fetch_body,
        (shape((ffw, width), BF16),),
        (lax.optimization_barrier((down_weight[0], within))[0],),
        flops=2 * slots * width * ffw,
        name="fetch",
        stay=(0,),
        scratch=(pltpu.SemaphoreType.DMA(()),),
    )
    if order:
        packed[LATE], weight = lax.optimization_barrier((packed[LATE], weight))
        arrived = [swap(rows, "expert", k) if k else rows for k, rows in zip(order, packed)]
    else:
        arrived = [exchange(packed[0])]
    replicas = [*range(2, n_dp), 1, 0]
    all_stored = [swap(stored, "dp", k) if k else stored for k in replicas]

    rows, prob, *weighted = kernel_call(
        functools.partial(weigh_body, replicas, order),
        (shape((slots, width), BF16), shape((slots, LANES), F32))
        + (shape((slots, chunk), BF16),) * n_dp,
        arrived,
        flops=2 * slots * width,
        name="weigh",
        scratch=(pltpu.VMEM((slots, width + LANES), F32),),
    )
    weighted = [swap(rows, "dp", k) if k else rows for k, rows in zip(replicas, weighted)]
    grad_act, table = kernel_call(
        functools.partial(act_body, experts, cap),
        (shape((slots, ffw), BF16), shape((experts, 8, LANES), F32)),
        (rows, prob, weight, stored),
        flops=2 * slots * width * ffw,
        name="act",
    )
    reweight = exchange(table)
    (grad_weight,) = kernel_call(
        functools.partial(gradient_body, n_dp),
        (shape((chunk, ffw), F32),),
        (*weighted, *all_stored),
        flops=2 * n_dp * slots * chunk * ffw,
        name="gradient",
    )
    reweight, grad_weight = lax.optimization_barrier((reweight, grad_weight))
    (grad_prob,) = kernel_call(
        functools.partial(pick_body, experts),
        (shape((1, tokens), F32),),
        (ids, within, reweight),
        name="pick",
    )
    return (grad_act[None, None], grad_weight[None], grad_prob.reshape(tokens, 1))


def solution(mesh):
    return jax.shard_map(
        functools.partial(shards, mesh.shape["dp"], mesh.shape["expert"]),
        mesh=mesh,
        in_specs=(
            P(("dp", "expert"), None),
            P(("dp", "expert"), None),
            P(("dp", "expert"), None),
            P("dp", "expert", None, None),
            P("expert", None, None),
        ),
        out_specs=(
            P("dp", "expert", None, None),
            P("expert", "dp", None),
            P(("dp", "expert"), None),
        ),
        check_vma=False,
    )
```

```python
import functools

import jax
import jax.numpy as jnp
from jax import lax
from jax.experimental import pallas as pl
from jax.experimental.pallas import tpu as pltpu
from jax.sharding import PartitionSpec as P

LANES = 128
F32 = jnp.float32
BF16 = jnp.bfloat16
ORDER = (6, 1, 7, 2, 4, 5, 3, 0)
LATE = 6


def kernel_call(body, outs, operands, name, flops=0, scratch=(), stay=()):
    nbytes = sum(a.size * a.dtype.itemsize for a in (*outs, *operands))
    vmem, hbm = pl.BlockSpec(memory_space=pltpu.VMEM), pl.BlockSpec(memory_space=pltpu.HBM)
    operands = [
        pltpu.with_memory_space_constraint(a, pltpu.HBM) if i in stay else a
        for i, a in enumerate(operands)
    ]
    return pl.pallas_call(
        body,
        out_shape=outs,
        in_specs=[hbm if i in stay else vmem for i in range(len(operands))],
        out_specs=[vmem] * len(outs),
        scratch_shapes=scratch,
        compiler_params=pltpu.CompilerParams(vmem_limit_bytes=16 * 2**20),
        cost_estimate=pl.CostEstimate(flops=flops, bytes_accessed=nbytes, transcendentals=0),
        name=name,
    )(*operands)


def shape(dims, kind):
    return jax.ShapeDtypeStruct(dims, kind)


def dot(a, b, dims=((1,), (0,)), precision=None):
    return lax.dot_general(
        a, b, (dims, ((), ())), preferred_element_type=F32, precision=precision
    )


def iota(dims, axis):
    return lax.broadcasted_iota(jnp.int32, dims, axis)


def place_body(experts, order, cap, *refs):
    (ids_hbm, prob_hbm, rows_hbm), refs = refs[:3], refs[3:]
    *chunk_refs, within_ref, ids_ref, prob_ref, rows_ref, sems = refs
    copies = [
        pltpu.make_async_copy(source, target, sems.at[i])
        for i, (source, target) in enumerate(
            ((ids_hbm, ids_ref), (prob_hbm, prob_ref), (rows_hbm, rows_ref))
        )
    ]
    for copy in copies:
        copy.start()
    tokens, width = rows_ref.shape
    copies[0].wait()
    ids = ids_ref[...]
    slots, rows = experts * cap, chunk_refs[0].shape[0]
    member = (iota((experts, tokens), 0) == ids).astype(F32)
    earlier = (iota((tokens, tokens), 0) < iota((tokens, tokens), 1)).astype(BF16)
    before = dot(member.astype(BF16), earlier)
    within = jnp.sum(before * member, axis=0, keepdims=True).astype(jnp.int32)
    within_ref[...] = within
    partner = ids ^ lax.axis_index("expert")
    place = 0
    for i, k in enumerate(order):
        place = jnp.where(partner == k, i, place)
    if not order:
        place = ids
    chosen = iota((slots, tokens), 0) == place * cap + within
    copies[1].wait()
    prob = jnp.sum(jnp.where(chosen, prob_ref[...].astype(F32), 0.0), axis=1, keepdims=True)
    chosen = chosen.astype(BF16)
    copies[2].wait()

    def put(columns, values):
        for i, ref in enumerate(chunk_refs):
            ref[:, columns] = values[i * rows : (i + 1) * rows].astype(BF16)

    step = 2 * LANES
    for c in range(0, width, step):
        put(slice(c, c + step), dot(chosen, rows_ref[:, c : c + step]))
    put(slice(width, width + LANES), jnp.broadcast_to(prob, (slots, LANES)))


def weigh_body(replicas, order, *refs):
    n_dp = len(replicas)
    *chunk_refs, rows_ref, prob_ref = refs[: -n_dp - 1]
    weighted_refs, all_ref = refs[-n_dp - 1 : -1], refs[-1]
    width = rows_ref.shape[1]
    chunk = width // n_dp
    size = chunk_refs[0].shape[0]
    for c in range(0, width + LANES, LANES):
        columns = slice(c, c + LANES)
        for k, ref in zip(order or (0,), chunk_refs):
            at = (lax.axis_index("expert") ^ k) * size if order else 0
            all_ref[pl.ds(at, size), columns] = ref[:, columns].astype(F32)
    prob = all_ref[:, width:]
    prob_ref[...] = prob
    replica = lax.axis_index("dp")
    for k, ref in zip(replicas, weighted_refs):
        for c in range(0, chunk, LANES):
            columns = pl.ds(pl.multiple_of((replica ^ k) * chunk + c, LANES), LANES)
            piece = all_ref[:, columns]
            rows_ref[:, columns] = piece.astype(BF16)
            ref[:, c : c + LANES] = (piece * prob).astype(BF16)


def fetch_body(weight_hbm, out_ref, sem):
    copy = pltpu.make_async_copy(weight_hbm, out_ref, sem)
    copy.start()
    copy.wait()


def by_source(column, experts, cap):
    slots = experts * cap
    spread = jnp.where(iota((slots, LANES), 1) == iota((slots, LANES), 0) % cap, column, 0.0)
    if cap % 8 == 0:
        return jnp.sum(spread.reshape(experts, cap, LANES), axis=1)
    owner = (iota((experts, slots), 0) == iota((experts, slots), 1) // cap).astype(F32)
    return dot(owner, spread, precision=lax.Precision.HIGHEST)


def act_body(experts, cap, rows_ref, prob_ref, weight_ref, stored_ref, act_ref, table_ref):
    backed = dot(rows_ref[...], weight_ref[...], ((1,), (1,)))
    act_ref[...] = (prob_ref[:, 0:1] * backed).astype(BF16)
    column = jnp.sum(backed * stored_ref[...].astype(F32), axis=1, keepdims=True)
    table = by_source(column, experts, cap)
    table_ref[...] = jnp.broadcast_to(table[:, None], table_ref.shape)


def gradient_body(n_dp, *refs):
    lhs = jnp.concatenate([ref[...] for ref in refs[:n_dp]], axis=0)
    rhs = jnp.concatenate([ref[...] for ref in refs[n_dp:-1]], axis=0)
    refs[-1][...] = dot(lhs, rhs, ((0,), (0,)))


def pick_body(experts, ids_ref, within_ref, table_ref, out_ref):
    ids = ids_ref[...]
    tokens = ids.shape[1]
    at = jnp.broadcast_to(within_ref[...], (experts, tokens))
    values = jnp.take_along_axis(table_ref[:, 0, :], at, axis=1, mode="promise_in_bounds")
    member = iota((experts, tokens), 0) == ids
    out_ref[...] = jnp.sum(jnp.where(member, values, 0.0), axis=0, keepdims=True)


def shards(n_dp, experts, grad_out, route_prob, expert_ids, saved_act, down_weight):
    slots, ffw = saved_act.shape[2:]
    cap = slots // experts
    tokens, width = grad_out.shape
    chunk = width // n_dp
    stored = saved_act[0, 0]
    order = ORDER if experts == len(ORDER) else ()
    chunks = max(len(order), 1)
    ids = expert_ids.reshape(1, tokens)
    prob_row = route_prob.reshape(1, tokens)

    def swap(array, axis, k):
        size = lax.axis_size(axis)
        return lax.ppermute(array, axis, [(r, r ^ k) for r in range(size)])

    def exchange(array):
        return lax.all_to_all(array, "expert", split_axis=0, concat_axis=0, tiled=True)

    *packed, within = kernel_call(
        functools.partial(place_body, experts, order, cap),
        (shape((slots // chunks, width + LANES), BF16),) * chunks + (shape((1, tokens), jnp.int32),),
        (ids, prob_row, grad_out),
        flops=2 * slots * tokens * width,
        name="place",
        stay=(0, 1, 2),
        scratch=(
            pltpu.VMEM((1, tokens), jnp.int32),
            pltpu.VMEM((1, tokens), BF16),
            pltpu.VMEM((tokens, width), BF16),
            pltpu.SemaphoreType.DMA((3,)),
        ),
    )
    (weight,) = kernel_call(
        fetch_body,
        (shape((ffw, width), BF16),),
        (lax.optimization_barrier((down_weight[0], within))[0],),
        flops=2 * slots * width * ffw,
        name="fetch",
        stay=(0,),
        scratch=(pltpu.SemaphoreType.DMA(()),),
    )
    if order:
        packed[LATE], weight = lax.optimization_barrier((packed[LATE], weight))
        arrived = [swap(rows, "expert", k) if k else rows for k, rows in zip(order, packed)]
    else:
        arrived = [exchange(packed[0])]
    replicas = [*range(2, n_dp), 1, 0]
    held, step = {0: stored}, n_dp // 2
    while step:
        held |= {k | step: swap(array, "dp", step) for k, array in held.items()}
        step //= 2
    all_stored = [held[k] for k in replicas]

    rows, prob, *weighted = kernel_call(
        functools.partial(weigh_body, replicas, order),
        (shape((slots, width), BF16), shape((slots, LANES), F32))
        + (shape((slots, chunk), BF16),) * n_dp,
        arrived,
        flops=2 * slots * width,
        name="weigh",
        scratch=(pltpu.VMEM((slots, width + LANES), F32),),
    )
    weighted = [swap(rows, "dp", k) if k else rows for k, rows in zip(replicas, weighted)]
    grad_act, table = kernel_call(
        functools.partial(act_body, experts, cap),
        (shape((slots, ffw), BF16), shape((experts, 8, LANES), F32)),
        (rows, prob, weight, stored),
        flops=2 * slots * width * ffw,
        name="act",
    )
    returned = exchange(table)
    (grad_weight,) = kernel_call(
        functools.partial(gradient_body, n_dp),
        (shape((chunk, ffw), F32),),
        (*weighted, *all_stored),
        flops=2 * n_dp * slots * chunk * ffw,
        name="gradient",
    )
    returned, grad_weight = lax.optimization_barrier((returned, grad_weight))
    (grad_prob,) = kernel_call(
        functools.partial(pick_body, experts),
        (shape((1, tokens), F32),),
        (ids, within, returned),
        name="pick",
    )
    return (grad_act[None, None], grad_weight[None], grad_prob.reshape(tokens, 1))


def solution(mesh):
    return jax.shard_map(
        functools.partial(shards, mesh.shape["dp"], mesh.shape["expert"]),
        mesh=mesh,
        in_specs=(
            P(("dp", "expert"), None),
            P(("dp", "expert"), None),
            P(("dp", "expert"), None),
            P("dp", "expert", None, None),
            P("expert", None, None),
        ),
        out_specs=(
            P("dp", "expert", None, None),
            P("expert", "dp", None),
            P(("dp", "expert"), None),
        ),
        check_vma=False,
    )
```

```python
import functools

import jax
import jax.numpy as jnp
from jax import lax
from jax.experimental import pallas as pl
from jax.experimental.pallas import tpu as pltpu
from jax.sharding import PartitionSpec as P

LANES = 128
F32 = jnp.float32
BF16 = jnp.bfloat16
ORDER = (4, 1, 5, 2, 6, 7, 3, 0)
LATE = 6


def kernel_call(body, outs, operands, name, flops=0, scratch=(), stay=()):
    nbytes = sum(a.size * a.dtype.itemsize for a in (*outs, *operands))
    vmem, hbm = pl.BlockSpec(memory_space=pltpu.VMEM), pl.BlockSpec(memory_space=pltpu.HBM)
    operands = [
        pltpu.with_memory_space_constraint(a, pltpu.HBM) if i in stay else a
        for i, a in enumerate(operands)
    ]
    return pl.pallas_call(
        body,
        out_shape=outs,
        in_specs=[hbm if i in stay else vmem for i in range(len(operands))],
        out_specs=[vmem] * len(outs),
        scratch_shapes=scratch,
        compiler_params=pltpu.CompilerParams(vmem_limit_bytes=16 * 2**20),
        cost_estimate=pl.CostEstimate(flops=flops, bytes_accessed=nbytes, transcendentals=0),
        name=name,
    )(*operands)


def shape(dims, kind):
    return jax.ShapeDtypeStruct(dims, kind)


def dot(a, b, dims=((1,), (0,)), precision=None):
    return lax.dot_general(
        a, b, (dims, ((), ())), preferred_element_type=F32, precision=precision
    )


def iota(dims, axis):
    return lax.broadcasted_iota(jnp.int32, dims, axis)


def place_body(experts, order, cap, *refs):
    (ids_hbm, prob_hbm, rows_hbm), refs = refs[:3], refs[3:]
    *chunk_refs, within_ref, ids_ref, prob_ref, rows_ref, sems = refs
    copies = [
        pltpu.make_async_copy(source, target, sems.at[i])
        for i, (source, target) in enumerate(
            ((ids_hbm, ids_ref), (prob_hbm, prob_ref), (rows_hbm, rows_ref))
        )
    ]
    for copy in copies:
        copy.start()
    tokens, width = rows_ref.shape
    copies[0].wait()
    ids = ids_ref[...]
    slots, rows = experts * cap, chunk_refs[0].shape[0]
    member = (iota((experts, tokens), 0) == ids).astype(F32)
    earlier = (iota((tokens, tokens), 0) < iota((tokens, tokens), 1)).astype(BF16)
    before = dot(member.astype(BF16), earlier)
    within = jnp.sum(before * member, axis=0, keepdims=True).astype(jnp.int32)
    within_ref[...] = within
    partner = ids ^ lax.axis_index("expert")
    place = 0
    for i, k in enumerate(order):
        place = jnp.where(partner == k, i, place)
    if not order:
        place = ids
    chosen = iota((slots, tokens), 0) == place * cap + within
    copies[1].wait()
    prob = jnp.sum(jnp.where(chosen, prob_ref[...].astype(F32), 0.0), axis=1, keepdims=True)
    chosen = chosen.astype(BF16)
    copies[2].wait()

    def put(columns, values):
        for i, ref in enumerate(chunk_refs):
            ref[:, columns] = values[i * rows : (i + 1) * rows].astype(BF16)

    step = 2 * LANES
    for c in range(0, width, step):
        put(slice(c, c + step), dot(chosen, rows_ref[:, c : c + step]))
    put(slice(width, width + LANES), jnp.broadcast_to(prob, (slots, LANES)))


def weigh_body(replicas, order, *refs):
    n_dp = len(replicas)
    chunk_refs, weighted_refs, all_ref = refs[: -n_dp - 1], refs[-n_dp - 1 : -1], refs[-1]
    chunk = weighted_refs[0].shape[1]
    width = chunk * n_dp
    size = chunk_refs[0].shape[0]
    for c in range(0, width + LANES, LANES):
        columns = slice(c, c + LANES)
        for k, ref in zip(order or (0,), chunk_refs):
            at = (lax.axis_index("expert") ^ k) * size if order else 0
            all_ref[pl.ds(at, size), columns] = ref[:, columns].astype(F32)
    prob = all_ref[:, width:]
    replica = lax.axis_index("dp")
    for k, ref in zip(replicas, weighted_refs):
        for c in range(0, chunk, LANES):
            columns = pl.ds(pl.multiple_of((replica ^ k) * chunk + c, LANES), LANES)
            piece = all_ref[:, columns]
            ref[:, c : c + LANES] = (piece * prob).astype(BF16)


def fetch_body(weight_hbm, out_ref, sem):
    copy = pltpu.make_async_copy(weight_hbm, out_ref, sem)
    copy.start()
    copy.wait()


def by_source(column, experts, cap):
    slots = experts * cap
    spread = jnp.where(iota((slots, LANES), 1) == iota((slots, LANES), 0) % cap, column, 0.0)
    if cap % 8 == 0:
        return jnp.sum(spread.reshape(experts, cap, LANES), axis=1)
    owner = (iota((experts, slots), 0) == iota((experts, slots), 1) // cap).astype(F32)
    return dot(owner, spread, precision=lax.Precision.HIGHEST)


def act_body(order, cap, experts, count, *refs):
    chunk_refs, (weight_ref, stored_ref), refs = refs[:count], refs[count : count + 2], refs[count + 2 :]
    *earlier_refs, act_ref, table_ref, stored_all_ref, act_all_ref = refs
    width, ffw = weight_ref.shape[1], weight_ref.shape[0]
    rows = jnp.concatenate([ref[:, :width].astype(F32) for ref in chunk_refs], axis=0)
    prob = jnp.concatenate([ref[:, width:].astype(F32) for ref in chunk_refs], axis=0)
    backed = dot(rows.astype(BF16), weight_ref[...], ((1,), (1,)))
    acts = prob[:, 0:1] * backed
    stored_all_ref[...] = stored_ref[...].astype(F32)
    table = jnp.zeros((experts, LANES), F32)
    last = len(earlier_refs) > 0 or not order
    if order:
        act_all_ref[...] = earlier_refs[0][...] if last else jnp.zeros_like(act_all_ref)
        table = earlier_refs[1][...] if last else table
    size = chunk_refs[0].shape[0]
    for i, k in enumerate(order or (0,)):
        source = lax.axis_index("expert") ^ k if order else 0
        mine = slice(i * size, (i + 1) * size)
        column = jnp.sum(
            backed[mine] * stored_all_ref[pl.ds(source * size, size), :], axis=1, keepdims=True
        )
        if order:
            row = by_source(column, 1, cap)
            table += jnp.where(iota((experts, LANES), 0) == source, row, 0.0)
        else:
            table = by_source(column, experts, cap)
        act_all_ref[pl.ds(source * size, size), :] = acts[mine]
    if last:
        act_ref[...] = act_all_ref[...].astype(BF16)
        table_ref[...] = jnp.broadcast_to(table[:, None], table_ref.shape)
    else:
        act_ref[...] = act_all_ref[...]
        table_ref[...] = table


def gradient_body(n_dp, *refs):
    lhs = jnp.concatenate([ref[...] for ref in refs[:n_dp]], axis=0)
    rhs = jnp.concatenate([ref[...] for ref in refs[n_dp:-1]], axis=0)
    refs[-1][...] = dot(lhs, rhs, ((0,), (0,)))


def pick_body(experts, ids_ref, within_ref, table_ref, out_ref):
    ids = ids_ref[...]
    tokens = ids.shape[1]
    at = jnp.broadcast_to(within_ref[...], (experts, tokens))
    values = jnp.take_along_axis(table_ref[:, 0, :], at, axis=1, mode="promise_in_bounds")
    member = iota((experts, tokens), 0) == ids
    out_ref[...] = jnp.sum(jnp.where(member, values, 0.0), axis=0, keepdims=True)


def shards(n_dp, experts, grad_out, route_prob, expert_ids, saved_act, down_weight):
    slots, ffw = saved_act.shape[2:]
    cap = slots // experts
    tokens, width = grad_out.shape
    chunk = width // n_dp
    stored = saved_act[0, 0]
    order = ORDER if experts == len(ORDER) else ()
    chunks = max(len(order), 1)
    ids = expert_ids.reshape(1, tokens)
    prob_row = route_prob.reshape(1, tokens)

    def swap(array, axis, k):
        size = lax.axis_size(axis)
        return lax.ppermute(array, axis, [(r, r ^ k) for r in range(size)])

    def exchange(array):
        return lax.all_to_all(array, "expert", split_axis=0, concat_axis=0, tiled=True)

    *packed, within = kernel_call(
        functools.partial(place_body, experts, order, cap),
        (shape((slots // chunks, width + LANES), BF16),) * chunks + (shape((1, tokens), jnp.int32),),
        (ids, prob_row, grad_out),
        flops=2 * slots * tokens * width,
        name="place",
        stay=(0, 1, 2),
        scratch=(
            pltpu.VMEM((1, tokens), jnp.int32),
            pltpu.VMEM((1, tokens), BF16),
            pltpu.VMEM((tokens, width), BF16),
            pltpu.SemaphoreType.DMA((3,)),
        ),
    )
    (weight,) = kernel_call(
        fetch_body,
        (shape((ffw, width), BF16),),
        (lax.optimization_barrier((down_weight[0], within))[0],),
        flops=2 * slots * width * ffw,
        name="fetch",
        stay=(0,),
        scratch=(pltpu.SemaphoreType.DMA(()),),
    )
    if order:
        packed[LATE], weight = lax.optimization_barrier((packed[LATE], weight))
        arrived = [swap(rows, "expert", k) if k else rows for k, rows in zip(order, packed)]
    else:
        arrived = [exchange(packed[0])]
    replicas = [*range(2, n_dp), 1, 0]
    all_stored = [swap(stored, "dp", k) if k else stored for k in replicas]


    def multiply(part, earlier, last):
        return kernel_call(
            functools.partial(act_body, order[part], cap, experts, len(arrived[part])),
            (shape((slots, ffw), BF16), shape((experts, 8, LANES), F32))
            if last
            else (shape((slots, ffw), F32), shape((experts, LANES), F32)),
            (*arrived[part], weight, saved_act[0, 0], *earlier),
            flops=2 * slots * width * ffw // 2,
            name="act",
            scratch=(pltpu.VMEM((slots, ffw), F32),) * 2,
        )

    early, late = slice(0, len(order) // 2), slice(len(order) // 2, None)
    earlier = ()
    if order:
        bound = lax.optimization_barrier((*multiply(early, (), False), *arrived[late]))
        earlier, arrived[late] = bound[:2], bound[2:]
    weighted = kernel_call(
        functools.partial(weigh_body, replicas, order),
        (shape((slots, chunk), BF16),) * n_dp,
        arrived,
        flops=2 * slots * width,
        name="weigh",
        scratch=(pltpu.VMEM((slots, width + LANES), F32),),
    )
    weighted = [swap(rows, "dp", k) if k else rows for k, rows in zip(replicas, weighted)]
    grad_act, table = multiply(late, earlier, True)
    returned = exchange(table)
    (grad_weight,) = kernel_call(
        functools.partial(gradient_body, n_dp),
        (shape((chunk, ffw), F32),),
        (*weighted, *all_stored),
        flops=2 * n_dp * slots * chunk * ffw,
        name="gradient",
    )
    returned, grad_weight = lax.optimization_barrier((returned, grad_weight))
    (grad_prob,) = kernel_call(
        functools.partial(pick_body, experts),
        (shape((1, tokens), F32),),
        (ids, within, returned),
        name="pick",
    )
    return (grad_act[None, None], grad_weight[None], grad_prob.reshape(tokens, 1))


def solution(mesh):
    return jax.shard_map(
        functools.partial(shards, mesh.shape["dp"], mesh.shape["expert"]),
        mesh=mesh,
        in_specs=(
            P(("dp", "expert"), None),
            P(("dp", "expert"), None),
            P(("dp", "expert"), None),
            P("dp", "expert", None, None),
            P("expert", None, None),
        ),
        out_specs=(
            P("dp", "expert", None, None),
            P("expert", "dp", None),
            P(("dp", "expert"), None),
        ),
        check_vma=False,
    )
```

```python
import functools

import jax
import jax.numpy as jnp
from jax import lax
from jax.experimental import pallas as pl
from jax.experimental.pallas import tpu as pltpu
from jax.sharding import PartitionSpec as P

LANES = 128
F32 = jnp.float32
BF16 = jnp.bfloat16
ORDER = (6, 1, 7, 2, 4, 5, 3, 0)


def kernel_call(body, outs, operands, name, flops=0, scratch=(), stay=()):
    nbytes = sum(a.size * a.dtype.itemsize for a in (*outs, *operands))
    vmem, hbm = pl.BlockSpec(memory_space=pltpu.VMEM), pl.BlockSpec(memory_space=pltpu.HBM)
    operands = [
        pltpu.with_memory_space_constraint(a, pltpu.HBM) if i in stay else a
        for i, a in enumerate(operands)
    ]
    return pl.pallas_call(
        body,
        out_shape=outs,
        in_specs=[hbm if i in stay else vmem for i in range(len(operands))],
        out_specs=[vmem] * len(outs),
        scratch_shapes=scratch,
        compiler_params=pltpu.CompilerParams(vmem_limit_bytes=16 * 2**20),
        cost_estimate=pl.CostEstimate(flops=flops, bytes_accessed=nbytes, transcendentals=0),
        name=name,
    )(*operands)


def shape(dims, kind):
    return jax.ShapeDtypeStruct(dims, kind)


def dot(a, b, dims=((1,), (0,)), precision=None):
    return lax.dot_general(
        a, b, (dims, ((), ())), preferred_element_type=F32, precision=precision
    )


def iota(dims, axis):
    return lax.broadcasted_iota(jnp.int32, dims, axis)


def place_body(experts, order, cap, *refs):
    (ids_hbm, prob_hbm, rows_hbm), refs = refs[:3], refs[3:]
    *chunk_refs, within_ref, ids_ref, prob_ref, rows_ref, sems = refs
    copies = [
        pltpu.make_async_copy(source, target, sems.at[i])
        for i, (source, target) in enumerate(
            ((ids_hbm, ids_ref), (prob_hbm, prob_ref), (rows_hbm, rows_ref))
        )
    ]
    for copy in copies:
        copy.start()
    tokens, width = rows_ref.shape
    copies[0].wait()
    ids = ids_ref[...]
    slots, rows = experts * cap, chunk_refs[0].shape[0]
    member = (iota((experts, tokens), 0) == ids).astype(F32)
    earlier = (iota((tokens, tokens), 0) < iota((tokens, tokens), 1)).astype(BF16)
    before = dot(member.astype(BF16), earlier)
    within = jnp.sum(before * member, axis=0, keepdims=True).astype(jnp.int32)
    within_ref[...] = within
    partner = ids ^ lax.axis_index("expert")
    place = 0
    for i, k in enumerate(order):
        place = jnp.where(partner == k, i, place)
    if not order:
        place = ids
    chosen = iota((slots, tokens), 0) == place * cap + within
    copies[1].wait()
    prob = jnp.sum(jnp.where(chosen, prob_ref[...].astype(F32), 0.0), axis=1, keepdims=True)
    chosen = chosen.astype(BF16)
    copies[2].wait()

    def put(columns, values):
        for i, ref in enumerate(chunk_refs):
            ref[:, columns] = values[i * rows : (i + 1) * rows].astype(BF16)

    step = 2 * LANES
    for c in range(0, width, step):
        put(slice(c, c + step), dot(chosen, rows_ref[:, c : c + step]))
    put(slice(width, width + LANES), jnp.broadcast_to(prob, (slots, LANES)))


def weigh_body(replicas, order, *refs):
    n_dp = len(replicas)
    chunk_refs, weighted_refs, all_ref = refs[: -n_dp - 1], refs[-n_dp - 1 : -1], refs[-1]
    chunk = weighted_refs[0].shape[1]
    width = chunk * n_dp
    size = chunk_refs[0].shape[0]
    for c in range(0, width + LANES, LANES):
        columns = slice(c, c + LANES)
        for k, ref in zip(order or (0,), chunk_refs):
            at = (lax.axis_index("expert") ^ k) * size if order else 0
            all_ref[pl.ds(at, size), columns] = ref[:, columns].astype(F32)
    prob = all_ref[:, width:]
    replica = lax.axis_index("dp")
    for k, ref in zip(replicas, weighted_refs):
        for c in range(0, chunk, LANES):
            columns = pl.ds(pl.multiple_of((replica ^ k) * chunk + c, LANES), LANES)
            piece = all_ref[:, columns]
            ref[:, c : c + LANES] = (piece * prob).astype(BF16)


def fetch_body(weight_hbm, out_ref, sem):
    copy = pltpu.make_async_copy(weight_hbm, out_ref, sem)
    copy.start()
    copy.wait()


def by_source(column, experts, cap):
    slots = experts * cap
    spread = jnp.where(iota((slots, LANES), 1) == iota((slots, LANES), 0) % cap, column, 0.0)
    if cap % 8 == 0:
        return jnp.sum(spread.reshape(experts, cap, LANES), axis=1)
    owner = (iota((experts, slots), 0) == iota((experts, slots), 1) // cap).astype(F32)
    return dot(owner, spread, precision=lax.Precision.HIGHEST)


def act_body(order, cap, experts, count, *refs):
    chunk_refs, (weight_ref, stored_ref), refs = refs[:count], refs[count : count + 2], refs[count + 2 :]
    *earlier_refs, act_ref, table_ref, stored_all_ref, act_all_ref = refs
    width, ffw = weight_ref.shape[1], weight_ref.shape[0]
    rows = jnp.concatenate([ref[:, :width].astype(F32) for ref in chunk_refs], axis=0)
    prob = jnp.concatenate([ref[:, width:].astype(F32) for ref in chunk_refs], axis=0)
    backed = dot(rows.astype(BF16), weight_ref[...], ((1,), (1,)))
    acts = prob[:, 0:1] * backed
    stored_all_ref[...] = stored_ref[...].astype(F32)
    table = jnp.zeros((experts, LANES), F32)
    last = len(earlier_refs) > 0 or not order
    if order:
        act_all_ref[...] = earlier_refs[0][...] if last else jnp.zeros_like(act_all_ref)
        table = earlier_refs[1][...] if last else table
    size = chunk_refs[0].shape[0]
    for i, k in enumerate(order or (0,)):
        source = lax.axis_index("expert") ^ k if order else 0
        mine = slice(i * size, (i + 1) * size)
        column = jnp.sum(
            backed[mine] * stored_all_ref[pl.ds(source * size, size), :], axis=1, keepdims=True
        )
        if order:
            row = by_source(column, 1, cap)
            table += jnp.where(iota((experts, LANES), 0) == source, row, 0.0)
        else:
            table = by_source(column, experts, cap)
        act_all_ref[pl.ds(source * size, size), :] = acts[mine]
    if last:
        act_ref[...] = act_all_ref[...].astype(BF16)
        table_ref[...] = jnp.broadcast_to(table[:, None], table_ref.shape)
    else:
        act_ref[...] = act_all_ref[...]
        table_ref[...] = table


def gradient_body(n_dp, *refs):
    lhs = jnp.concatenate([ref[...] for ref in refs[:n_dp]], axis=0)
    rhs = jnp.concatenate([ref[...] for ref in refs[n_dp:-1]], axis=0)
    refs[-1][...] = dot(lhs, rhs, ((0,), (0,)))


def pick_body(experts, ids_ref, within_ref, table_ref, out_ref):
    ids = ids_ref[...]
    tokens = ids.shape[1]
    at = jnp.broadcast_to(within_ref[...], (experts, tokens))
    values = jnp.take_along_axis(table_ref[:, 0, :], at, axis=1, mode="promise_in_bounds")
    member = iota((experts, tokens), 0) == ids
    out_ref[...] = jnp.sum(jnp.where(member, values, 0.0), axis=0, keepdims=True)


def shards(n_dp, experts, grad_out, route_prob, expert_ids, saved_act, down_weight):
    slots, ffw = saved_act.shape[2:]
    cap = slots // experts
    tokens, width = grad_out.shape
    chunk = width // n_dp
    stored = saved_act[0, 0]
    order = ORDER if experts == len(ORDER) else ()
    chunks = max(len(order), 1)
    ids = expert_ids.reshape(1, tokens)
    prob_row = route_prob.reshape(1, tokens)

    def swap(array, axis, k):
        size = lax.axis_size(axis)
        return lax.ppermute(array, axis, [(r, r ^ k) for r in range(size)])

    def exchange(array):
        return lax.all_to_all(array, "expert", split_axis=0, concat_axis=0, tiled=True)

    *packed, within = kernel_call(
        functools.partial(place_body, experts, order, cap),
        (shape((slots // chunks, width + LANES), BF16),) * chunks + (shape((1, tokens), jnp.int32),),
        (ids, prob_row, grad_out),
        flops=2 * slots * tokens * width,
        name="place",
        stay=(0, 1, 2),
        scratch=(
            pltpu.VMEM((1, tokens), jnp.int32),
            pltpu.VMEM((1, tokens), BF16),
            pltpu.VMEM((tokens, width), BF16),
            pltpu.SemaphoreType.DMA((3,)),
        ),
    )
    if order:
        arrived = [swap(rows, "expert", k) if k else rows for k, rows in zip(order, packed)]
    else:
        arrived = [exchange(packed[0])]
    (weight,) = kernel_call(
        fetch_body,
        (shape((ffw, width), BF16),),
        (lax.optimization_barrier((down_weight[0], within))[0],),
        flops=2 * slots * width * ffw,
        name="fetch",
        stay=(0,),
        scratch=(pltpu.SemaphoreType.DMA(()),),
    )
    replicas = [*range(2, n_dp), 1, 0]
    all_stored = [swap(stored, "dp", k) if k else stored for k in replicas]


    def multiply(part, earlier, last):
        return kernel_call(
            functools.partial(act_body, order[part], cap, experts, len(arrived[part])),
            (shape((slots, ffw), BF16), shape((experts, 8, LANES), F32))
            if last
            else (shape((slots, ffw), F32), shape((experts, LANES), F32)),
            (*arrived[part], weight, saved_act[0, 0], *earlier),
            flops=2 * slots * width * ffw // 2,
            name="act",
            scratch=(pltpu.VMEM((slots, ffw), F32),) * 2,
        )

    early, late = slice(0, len(order) // 2), slice(len(order) // 2, None)
    earlier = ()
    if order:
        bound = lax.optimization_barrier((*multiply(early, (), False), *arrived[late]))
        earlier, arrived[late] = bound[:2], bound[2:]
    weighted = kernel_call(
        functools.partial(weigh_body, replicas, order),
        (shape((slots, chunk), BF16),) * n_dp,
        arrived,
        flops=2 * slots * width,
        name="weigh",
        scratch=(pltpu.VMEM((slots, width + LANES), F32),),
    )
    weighted = [swap(rows, "dp", k) if k else rows for k, rows in zip(replicas, weighted)]
    grad_act, table = multiply(late, earlier, True)
    returned = exchange(table)
    (grad_weight,) = kernel_call(
        functools.partial(gradient_body, n_dp),
        (shape((chunk, ffw), F32),),
        (*weighted, *all_stored),
        flops=2 * n_dp * slots * chunk * ffw,
        name="gradient",
    )
    returned, grad_weight = lax.optimization_barrier((returned, grad_weight))
    (grad_prob,) = kernel_call(
        functools.partial(pick_body, experts),
        (shape((1, tokens), F32),),
        (ids, within, returned),
        name="pick",
    )
    return (grad_act[None, None], grad_weight[None], grad_prob.reshape(tokens, 1))


def solution(mesh):
    return jax.shard_map(
        functools.partial(shards, mesh.shape["dp"], mesh.shape["expert"]),
        mesh=mesh,
        in_specs=(
            P(("dp", "expert"), None),
            P(("dp", "expert"), None),
            P(("dp", "expert"), None),
            P("dp", "expert", None, None),
            P("expert", None, None),
        ),
        out_specs=(
            P("dp", "expert", None, None),
            P("expert", "dp", None),
            P(("dp", "expert"), None),
        ),
        check_vma=False,
    )
```

```python
import functools

import jax
import jax.numpy as jnp
from jax import lax
from jax.experimental import pallas as pl
from jax.experimental.pallas import tpu as pltpu
from jax.sharding import PartitionSpec as P

LANES = 128
F32 = jnp.float32
BF16 = jnp.bfloat16
ORDER = (6, 1, 7, 2, 4, 5, 3, 0)


def kernel_call(body, outs, operands, name, flops=0, scratch=(), stay=()):
    nbytes = sum(a.size * a.dtype.itemsize for a in (*outs, *operands))
    vmem, hbm = pl.BlockSpec(memory_space=pltpu.VMEM), pl.BlockSpec(memory_space=pltpu.HBM)
    operands = [
        pltpu.with_memory_space_constraint(a, pltpu.HBM) if i in stay else a
        for i, a in enumerate(operands)
    ]
    return pl.pallas_call(
        body,
        out_shape=outs,
        in_specs=[hbm if i in stay else vmem for i in range(len(operands))],
        out_specs=[vmem] * len(outs),
        scratch_shapes=scratch,
        compiler_params=pltpu.CompilerParams(vmem_limit_bytes=16 * 2**20),
        cost_estimate=pl.CostEstimate(flops=flops, bytes_accessed=nbytes, transcendentals=0),
        name=name,
    )(*operands)


def shape(dims, kind):
    return jax.ShapeDtypeStruct(dims, kind)


def dot(a, b, dims=((1,), (0,)), precision=None):
    return lax.dot_general(
        a, b, (dims, ((), ())), preferred_element_type=F32, precision=precision
    )


def iota(dims, axis):
    return lax.broadcasted_iota(jnp.int32, dims, axis)


def place_body(experts, order, cap, *refs):
    (ids_hbm, prob_hbm, rows_hbm), refs = refs[:3], refs[3:]
    *chunk_refs, within_ref, ids_ref, prob_ref, rows_ref, sems = refs
    copies = [
        pltpu.make_async_copy(source, target, sems.at[i])
        for i, (source, target) in enumerate(
            ((ids_hbm, ids_ref), (prob_hbm, prob_ref), (rows_hbm, rows_ref))
        )
    ]
    for copy in copies:
        copy.start()
    tokens, width = rows_ref.shape
    copies[0].wait()
    ids = ids_ref[...]
    slots, rows = experts * cap, chunk_refs[0].shape[0]
    member = (iota((experts, tokens), 0) == ids).astype(F32)
    earlier = (iota((tokens, tokens), 0) < iota((tokens, tokens), 1)).astype(BF16)
    before = dot(member.astype(BF16), earlier)
    within = jnp.sum(before * member, axis=0, keepdims=True).astype(jnp.int32)
    within_ref[...] = within
    partner = ids ^ lax.axis_index("expert")
    place = 0
    for i, k in enumerate(order):
        place = jnp.where(partner == k, i, place)
    if not order:
        place = ids
    chosen = iota((slots, tokens), 0) == place * cap + within
    copies[1].wait()
    prob = jnp.sum(jnp.where(chosen, prob_ref[...].astype(F32), 0.0), axis=1, keepdims=True)
    chosen = chosen.astype(BF16)
    copies[2].wait()

    def put(columns, values):
        for i, ref in enumerate(chunk_refs):
            ref[:, columns] = values[i * rows : (i + 1) * rows].astype(BF16)

    step = 2 * LANES
    for c in range(0, width, step):
        put(slice(c, c + step), dot(chosen, rows_ref[:, c : c + step]))
    put(slice(width, width + LANES), jnp.broadcast_to(prob, (slots, LANES)))


def weigh_body(replicas, order, *refs):
    n_dp = len(replicas)
    *chunk_refs, rows_ref, prob_ref = refs[: -n_dp - 1]
    weighted_refs, all_ref = refs[-n_dp - 1 : -1], refs[-1]
    width = rows_ref.shape[1]
    chunk = width // n_dp
    size = chunk_refs[0].shape[0]
    for c in range(0, width + LANES, LANES):
        columns = slice(c, c + LANES)
        for k, ref in zip(order or (0,), chunk_refs):
            at = (lax.axis_index("expert") ^ k) * size if order else 0
            all_ref[pl.ds(at, size), columns] = ref[:, columns].astype(F32)
    prob = all_ref[:, width:]
    prob_ref[...] = prob
    replica = lax.axis_index("dp")
    for k, ref in zip(replicas, weighted_refs):
        for c in range(0, chunk, LANES):
            columns = pl.ds(pl.multiple_of((replica ^ k) * chunk + c, LANES), LANES)
            piece = all_ref[:, columns]
            rows_ref[:, columns] = piece.astype(BF16)
            ref[:, c : c + LANES] = (piece * prob).astype(BF16)


def fetch_body(weight_hbm, out_ref, sem):
    copy = pltpu.make_async_copy(weight_hbm, out_ref, sem)
    copy.start()
    copy.wait()


def by_source(column, experts, cap):
    slots = experts * cap
    spread = jnp.where(iota((slots, LANES), 1) == iota((slots, LANES), 0) % cap, column, 0.0)
    if cap % 8 == 0:
        return jnp.sum(spread.reshape(experts, cap, LANES), axis=1)
    owner = (iota((experts, slots), 0) == iota((experts, slots), 1) // cap).astype(F32)
    return dot(owner, spread, precision=lax.Precision.HIGHEST)


def act_body(experts, cap, rows_ref, prob_ref, weight_ref, stored_ref, act_ref, table_ref):
    backed = dot(rows_ref[...], weight_ref[...], ((1,), (1,)))
    act_ref[...] = (prob_ref[:, 0:1] * backed).astype(BF16)
    column = jnp.sum(backed * stored_ref[...].astype(F32), axis=1, keepdims=True)
    table = by_source(column, experts, cap)
    table_ref[...] = jnp.broadcast_to(table[:, None], table_ref.shape)


def gradient_body(n_dp, *refs):
    lhs = jnp.concatenate([ref[...] for ref in refs[:n_dp]], axis=0)
    rhs = jnp.concatenate([ref[...] for ref in refs[n_dp:-1]], axis=0)
    refs[-1][...] = dot(lhs, rhs, ((0,), (0,)))


def pick_body(experts, ids_ref, within_ref, table_ref, out_ref):
    ids = ids_ref[...]
    tokens = ids.shape[1]
    at = jnp.broadcast_to(within_ref[...], (experts, tokens))
    values = jnp.take_along_axis(table_ref[:, 0, :], at, axis=1, mode="promise_in_bounds")
    member = iota((experts, tokens), 0) == ids
    out_ref[...] = jnp.sum(jnp.where(member, values, 0.0), axis=0, keepdims=True)


def shards(n_dp, experts, grad_out, route_prob, expert_ids, saved_act, down_weight):
    slots, ffw = saved_act.shape[2:]
    cap = slots // experts
    tokens, width = grad_out.shape
    chunk = width // n_dp
    stored = saved_act[0, 0]
    order = ORDER if experts == len(ORDER) else ()
    chunks = max(len(order), 1)
    ids = expert_ids.reshape(1, tokens)
    prob_row = route_prob.reshape(1, tokens)

    def swap(array, axis, k):
        size = lax.axis_size(axis)
        return lax.ppermute(array, axis, [(r, r ^ k) for r in range(size)])

    def exchange(array):
        return lax.all_to_all(array, "expert", split_axis=0, concat_axis=0, tiled=True)

    *packed, within = kernel_call(
        functools.partial(place_body, experts, order, cap),
        (shape((slots // chunks, width + LANES), BF16),) * chunks + (shape((1, tokens), jnp.int32),),
        (ids, prob_row, grad_out),
        flops=2 * slots * tokens * width,
        name="place",
        stay=(0, 1, 2),
        scratch=(
            pltpu.VMEM((1, tokens), jnp.int32),
            pltpu.VMEM((1, tokens), BF16),
            pltpu.VMEM((tokens, width), BF16),
            pltpu.SemaphoreType.DMA((3,)),
        ),
    )
    (weight,) = kernel_call(
        fetch_body,
        (shape((ffw, width), BF16),),
        (lax.optimization_barrier((down_weight[0], within))[0],),
        flops=2 * slots * width * ffw,
        name="fetch",
        stay=(0,),
        scratch=(pltpu.SemaphoreType.DMA(()),),
    )
    if order:
        arrived = [swap(rows, "expert", k) if k else rows for k, rows in zip(order, packed)]
    else:
        arrived = [exchange(packed[0])]
    replicas = [*range(2, n_dp), 1, 0]
    late, weight = lax.optimization_barrier((stored, weight))
    all_stored = [
        swap(stored if k == replicas[0] else late, "dp", k) if k else stored for k in replicas
    ]

    rows, prob, *weighted = kernel_call(
        functools.partial(weigh_body, replicas, order),
        (shape((slots, width), BF16), shape((slots, LANES), F32))
        + (shape((slots, chunk), BF16),) * n_dp,
        arrived,
        flops=2 * slots * width,
        name="weigh",
        scratch=(pltpu.VMEM((slots, width + LANES), F32),),
    )
    weighted = [swap(rows, "dp", k) if k else rows for k, rows in zip(replicas, weighted)]
    grad_act, table = kernel_call(
        functools.partial(act_body, experts, cap),
        (shape((slots, ffw), BF16), shape((experts, 8, LANES), F32)),
        (rows, prob, weight, stored),
        flops=2 * slots * width * ffw,
        name="act",
    )
    returned = exchange(table)
    (grad_weight,) = kernel_call(
        functools.partial(gradient_body, n_dp),
        (shape((chunk, ffw), F32),),
        (*weighted, *all_stored),
        flops=2 * n_dp * slots * chunk * ffw,
        name="gradient",
    )
    returned, grad_weight = lax.optimization_barrier((returned, grad_weight))
    (grad_prob,) = kernel_call(
        functools.partial(pick_body, experts),
        (shape((1, tokens), F32),),
        (ids, within, returned),
        name="pick",
    )
    return (grad_act[None, None], grad_weight[None], grad_prob.reshape(tokens, 1))


def solution(mesh):
    return jax.shard_map(
        functools.partial(shards, mesh.shape["dp"], mesh.shape["expert"]),
        mesh=mesh,
        in_specs=(
            P(("dp", "expert"), None),
            P(("dp", "expert"), None),
            P(("dp", "expert"), None),
            P("dp", "expert", None, None),
            P("expert", None, None),
        ),
        out_specs=(
            P("dp", "expert", None, None),
            P("expert", "dp", None),
            P(("dp", "expert"), None),
        ),
        check_vma=False,
    )
```

```python
import functools

import jax
import jax.numpy as jnp
from jax import lax
from jax.experimental import pallas as pl
from jax.experimental.pallas import tpu as pltpu
from jax.sharding import PartitionSpec as P

LANES = 128
F32 = jnp.float32
BF16 = jnp.bfloat16
ORDER = (6, 1, 2, 7, 4, 5, 3, 0)


def kernel_call(body, outs, operands, name, flops=0, scratch=(), stay=()):
    nbytes = sum(a.size * a.dtype.itemsize for a in (*outs, *operands))
    vmem, hbm = pl.BlockSpec(memory_space=pltpu.VMEM), pl.BlockSpec(memory_space=pltpu.HBM)
    operands = [
        pltpu.with_memory_space_constraint(a, pltpu.HBM) if i in stay else a
        for i, a in enumerate(operands)
    ]
    return pl.pallas_call(
        body,
        out_shape=outs,
        in_specs=[hbm if i in stay else vmem for i in range(len(operands))],
        out_specs=[vmem] * len(outs),
        scratch_shapes=scratch,
        compiler_params=pltpu.CompilerParams(vmem_limit_bytes=16 * 2**20),
        cost_estimate=pl.CostEstimate(flops=flops, bytes_accessed=nbytes, transcendentals=0),
        name=name,
    )(*operands)


def shape(dims, kind):
    return jax.ShapeDtypeStruct(dims, kind)


def dot(a, b, dims=((1,), (0,)), precision=None):
    return lax.dot_general(
        a, b, (dims, ((), ())), preferred_element_type=F32, precision=precision
    )


def iota(dims, axis):
    return lax.broadcasted_iota(jnp.int32, dims, axis)


def place_body(experts, order, cap, *refs):
    (ids_hbm, prob_hbm, rows_hbm), refs = refs[:3], refs[3:]
    *chunk_refs, within_ref, ids_ref, prob_ref, rows_ref, sems = refs
    copies = [
        pltpu.make_async_copy(source, target, sems.at[i])
        for i, (source, target) in enumerate(
            ((ids_hbm, ids_ref), (prob_hbm, prob_ref), (rows_hbm, rows_ref))
        )
    ]
    for copy in copies:
        copy.start()
    tokens, width = rows_ref.shape
    copies[0].wait()
    ids = ids_ref[...]
    slots, rows = experts * cap, chunk_refs[0].shape[0]
    member = (iota((experts, tokens), 0) == ids).astype(F32)
    earlier = (iota((tokens, tokens), 0) < iota((tokens, tokens), 1)).astype(BF16)
    before = dot(member.astype(BF16), earlier)
    within = jnp.sum(before * member, axis=0, keepdims=True).astype(jnp.int32)
    within_ref[...] = within
    partner = ids ^ lax.axis_index("expert")
    place = 0
    for i, k in enumerate(order):
        place = jnp.where(partner == k, i, place)
    if not order:
        place = ids
    chosen = iota((slots, tokens), 0) == place * cap + within
    copies[1].wait()
    prob = jnp.sum(jnp.where(chosen, prob_ref[...].astype(F32), 0.0), axis=1, keepdims=True)
    chosen = chosen.astype(BF16)
    copies[2].wait()

    def put(columns, values):
        for i, ref in enumerate(chunk_refs):
            ref[:, columns] = values[i * rows : (i + 1) * rows].astype(BF16)

    step = 2 * LANES
    for c in range(0, width, step):
        put(slice(c, c + step), dot(chosen, rows_ref[:, c : c + step]))
    put(slice(width, width + LANES), jnp.broadcast_to(prob, (slots, LANES)))


def weigh_body(replicas, order, *refs):
    n_dp = len(replicas)
    *chunk_refs, rows_ref, prob_ref = refs[: -n_dp - 1]
    weighted_refs, all_ref = refs[-n_dp - 1 : -1], refs[-1]
    width = rows_ref.shape[1]
    chunk = width // n_dp
    size = chunk_refs[0].shape[0]
    for c in range(0, width + LANES, LANES):
        columns = slice(c, c + LANES)
        for k, ref in zip(order or (0,), chunk_refs):
            at = (lax.axis_index("expert") ^ k) * size if order else 0
            all_ref[pl.ds(at, size), columns] = ref[:, columns].astype(F32)
    prob = all_ref[:, width:]
    prob_ref[...] = prob
    replica = lax.axis_index("dp")
    for k, ref in zip(replicas, weighted_refs):
        for c in range(0, chunk, LANES):
            columns = pl.ds(pl.multiple_of((replica ^ k) * chunk + c, LANES), LANES)
            piece = all_ref[:, columns]
            rows_ref[:, columns] = piece.astype(BF16)
            ref[:, c : c + LANES] = (piece * prob).astype(BF16)


def fetch_body(weight_hbm, out_ref, sem):
    copy = pltpu.make_async_copy(weight_hbm, out_ref, sem)
    copy.start()
    copy.wait()


def by_source(column, experts, cap):
    slots = experts * cap
    spread = jnp.where(iota((slots, LANES), 1) == iota((slots, LANES), 0) % cap, column, 0.0)
    if cap % 8 == 0:
        return jnp.sum(spread.reshape(experts, cap, LANES), axis=1)
    owner = (iota((experts, slots), 0) == iota((experts, slots), 1) // cap).astype(F32)
    return dot(owner, spread, precision=lax.Precision.HIGHEST)


def act_body(experts, cap, rows_ref, prob_ref, weight_ref, stored_ref, act_ref, table_ref):
    backed = dot(rows_ref[...], weight_ref[...], ((1,), (1,)))
    act_ref[...] = (prob_ref[:, 0:1] * backed).astype(BF16)
    column = jnp.sum(backed * stored_ref[...].astype(F32), axis=1, keepdims=True)
    table = by_source(column, experts, cap)
    table_ref[...] = jnp.broadcast_to(table[:, None], table_ref.shape)


def gradient_body(n_dp, *refs):
    lhs = jnp.concatenate([ref[...] for ref in refs[:n_dp]], axis=0)
    rhs = jnp.concatenate([ref[...] for ref in refs[n_dp:-1]], axis=0)
    refs[-1][...] = dot(lhs, rhs, ((0,), (0,)))


def pick_body(experts, ids_ref, within_ref, table_ref, out_ref):
    ids = ids_ref[...]
    tokens = ids.shape[1]
    at = jnp.broadcast_to(within_ref[...], (experts, tokens))
    values = jnp.take_along_axis(table_ref[:, 0, :], at, axis=1, mode="promise_in_bounds")
    member = iota((experts, tokens), 0) == ids
    out_ref[...] = jnp.sum(jnp.where(member, values, 0.0), axis=0, keepdims=True)


def shards(n_dp, experts, grad_out, route_prob, expert_ids, saved_act, down_weight):
    slots, ffw = saved_act.shape[2:]
    cap = slots // experts
    tokens, width = grad_out.shape
    chunk = width // n_dp
    stored = saved_act[0, 0]
    order = ORDER if experts == len(ORDER) else ()
    chunks = max(len(order), 1)
    ids = expert_ids.reshape(1, tokens)
    prob_row = route_prob.reshape(1, tokens)

    def swap(array, axis, k):
        size = lax.axis_size(axis)
        return lax.ppermute(array, axis, [(r, r ^ k) for r in range(size)])

    def exchange(array):
        return lax.all_to_all(array, "expert", split_axis=0, concat_axis=0, tiled=True)

    *packed, within = kernel_call(
        functools.partial(place_body, experts, order, cap),
        (shape((slots // chunks, width + LANES), BF16),) * chunks + (shape((1, tokens), jnp.int32),),
        (ids, prob_row, grad_out),
        flops=2 * slots * tokens * width,
        name="place",
        stay=(0, 1, 2),
        scratch=(
            pltpu.VMEM((1, tokens), jnp.int32),
            pltpu.VMEM((1, tokens), BF16),
            pltpu.VMEM((tokens, width), BF16),
            pltpu.SemaphoreType.DMA((3,)),
        ),
    )
    (weight,) = kernel_call(
        fetch_body,
        (shape((ffw, width), BF16),),
        (lax.optimization_barrier((down_weight[0], within))[0],),
        flops=2 * slots * width * ffw,
        name="fetch",
        stay=(0,),
        scratch=(pltpu.SemaphoreType.DMA(()),),
    )
    if order:
        arrived = [swap(rows, "expert", k) if k else rows for k, rows in zip(order, packed)]
    else:
        arrived = [exchange(packed[0])]
    replicas = [*range(2, n_dp), 1, 0]
    late, weight = lax.optimization_barrier((stored, weight))
    all_stored = [
        swap(stored if k == replicas[0] else late, "dp", k) if k else stored for k in replicas
    ]

    rows, prob, *weighted = kernel_call(
        functools.partial(weigh_body, replicas, order),
        (shape((slots, width), BF16), shape((slots, LANES), F32))
        + (shape((slots, chunk), BF16),) * n_dp,
        arrived,
        flops=2 * slots * width,
        name="weigh",
        scratch=(pltpu.VMEM((slots, width + LANES), F32),),
    )
    weighted = [swap(rows, "dp", k) if k else rows for k, rows in zip(replicas, weighted)]
    grad_act, table = kernel_call(
        functools.partial(act_body, experts, cap),
        (shape((slots, ffw), BF16), shape((experts, 8, LANES), F32)),
        (rows, prob, weight, stored),
        flops=2 * slots * width * ffw,
        name="act",
    )
    returned = exchange(table)
    (grad_weight,) = kernel_call(
        functools.partial(gradient_body, n_dp),
        (shape((chunk, ffw), F32),),
        (*weighted, *all_stored),
        flops=2 * n_dp * slots * chunk * ffw,
        name="gradient",
    )
    returned, grad_weight = lax.optimization_barrier((returned, grad_weight))
    (grad_prob,) = kernel_call(
        functools.partial(pick_body, experts),
        (shape((1, tokens), F32),),
        (ids, within, returned),
        name="pick",
    )
    return (grad_act[None, None], grad_weight[None], grad_prob.reshape(tokens, 1))


def solution(mesh):
    return jax.shard_map(
        functools.partial(shards, mesh.shape["dp"], mesh.shape["expert"]),
        mesh=mesh,
        in_specs=(
            P(("dp", "expert"), None),
            P(("dp", "expert"), None),
            P(("dp", "expert"), None),
            P("dp", "expert", None, None),
            P("expert", None, None),
        ),
        out_specs=(
            P("dp", "expert", None, None),
            P("expert", "dp", None),
            P(("dp", "expert"), None),
        ),
        check_vma=False,
    )
```

```python
import functools

import jax
import jax.numpy as jnp
from jax import lax
from jax.experimental import pallas as pl
from jax.experimental.pallas import tpu as pltpu
from jax.sharding import PartitionSpec as P

LANES = 128
F32 = jnp.float32
BF16 = jnp.bfloat16
ORDER = (6, 1, 2, 7, 5, 4, 3, 0)


def kernel_call(body, outs, operands, name, flops=0, scratch=(), stay=()):
    nbytes = sum(a.size * a.dtype.itemsize for a in (*outs, *operands))
    vmem, hbm = pl.BlockSpec(memory_space=pltpu.VMEM), pl.BlockSpec(memory_space=pltpu.HBM)
    operands = [
        pltpu.with_memory_space_constraint(a, pltpu.HBM) if i in stay else a
        for i, a in enumerate(operands)
    ]
    return pl.pallas_call(
        body,
        out_shape=outs,
        in_specs=[hbm if i in stay else vmem for i in range(len(operands))],
        out_specs=[vmem] * len(outs),
        scratch_shapes=scratch,
        compiler_params=pltpu.CompilerParams(vmem_limit_bytes=16 * 2**20),
        cost_estimate=pl.CostEstimate(flops=flops, bytes_accessed=nbytes, transcendentals=0),
        name=name,
    )(*operands)


def shape(dims, kind):
    return jax.ShapeDtypeStruct(dims, kind)


def dot(a, b, dims=((1,), (0,)), precision=None):
    return lax.dot_general(
        a, b, (dims, ((), ())), preferred_element_type=F32, precision=precision
    )


def iota(dims, axis):
    return lax.broadcasted_iota(jnp.int32, dims, axis)


def place_body(experts, order, cap, *refs):
    (ids_hbm, prob_hbm, rows_hbm), refs = refs[:3], refs[3:]
    *chunk_refs, within_ref, ids_ref, prob_ref, rows_ref, sems = refs
    copies = [
        pltpu.make_async_copy(source, target, sems.at[i])
        for i, (source, target) in enumerate(
            ((ids_hbm, ids_ref), (prob_hbm, prob_ref), (rows_hbm, rows_ref))
        )
    ]
    for copy in copies:
        copy.start()
    tokens, width = rows_ref.shape
    copies[0].wait()
    ids = ids_ref[...]
    slots, rows = experts * cap, chunk_refs[0].shape[0]
    member = (iota((experts, tokens), 0) == ids).astype(F32)
    earlier = (iota((tokens, tokens), 0) < iota((tokens, tokens), 1)).astype(BF16)
    before = dot(member.astype(BF16), earlier)
    within = jnp.sum(before * member, axis=0, keepdims=True).astype(jnp.int32)
    within_ref[...] = within
    partner = ids ^ lax.axis_index("expert")
    place = 0
    for i, k in enumerate(order):
        place = jnp.where(partner == k, i, place)
    if not order:
        place = ids
    chosen = iota((slots, tokens), 0) == place * cap + within
    copies[1].wait()
    prob = jnp.sum(jnp.where(chosen, prob_ref[...].astype(F32), 0.0), axis=1, keepdims=True)
    chosen = chosen.astype(BF16)
    copies[2].wait()

    def put(columns, values):
        for i, ref in enumerate(chunk_refs):
            ref[:, columns] = values[i * rows : (i + 1) * rows].astype(BF16)

    step = 2 * LANES
    for c in range(0, width, step):
        put(slice(c, c + step), dot(chosen, rows_ref[:, c : c + step]))
    put(slice(width, width + LANES), jnp.broadcast_to(prob, (slots, LANES)))


def weigh_body(replicas, order, *refs):
    n_dp = len(replicas)
    *chunk_refs, rows_ref, prob_ref = refs[: -n_dp - 1]
    weighted_refs, all_ref = refs[-n_dp - 1 : -1], refs[-1]
    width = rows_ref.shape[1]
    chunk = width // n_dp
    size = chunk_refs[0].shape[0]
    for c in range(0, width + LANES, LANES):
        columns = slice(c, c + LANES)
        for k, ref in zip(order or (0,), chunk_refs):
            at = (lax.axis_index("expert") ^ k) * size if order else 0
            all_ref[pl.ds(at, size), columns] = ref[:, columns].astype(F32)
    prob = all_ref[:, width:]
    prob_ref[...] = prob
    replica = lax.axis_index("dp")
    for k, ref in zip(replicas, weighted_refs):
        for c in range(0, chunk, LANES):
            columns = pl.ds(pl.multiple_of((replica ^ k) * chunk + c, LANES), LANES)
            piece = all_ref[:, columns]
            rows_ref[:, columns] = piece.astype(BF16)
            ref[:, c : c + LANES] = (piece * prob).astype(BF16)


def fetch_body(weight_hbm, out_ref, sem):
    copy = pltpu.make_async_copy(weight_hbm, out_ref, sem)
    copy.start()
    copy.wait()


def by_source(column, experts, cap):
    slots = experts * cap
    spread = jnp.where(iota((slots, LANES), 1) == iota((slots, LANES), 0) % cap, column, 0.0)
    if cap % 8 == 0:
        return jnp.sum(spread.reshape(experts, cap, LANES), axis=1)
    owner = (iota((experts, slots), 0) == iota((experts, slots), 1) // cap).astype(F32)
    return dot(owner, spread, precision=lax.Precision.HIGHEST)


def act_body(experts, cap, rows_ref, prob_ref, weight_ref, stored_ref, act_ref, table_ref):
    backed = dot(rows_ref[...], weight_ref[...], ((1,), (1,)))
    act_ref[...] = (prob_ref[:, 0:1] * backed).astype(BF16)
    column = jnp.sum(backed * stored_ref[...].astype(F32), axis=1, keepdims=True)
    table = by_source(column, experts, cap)
    table_ref[...] = jnp.broadcast_to(table[:, None], table_ref.shape)


def gradient_body(n_dp, *refs):
    lhs = jnp.concatenate([ref[...] for ref in refs[:n_dp]], axis=0)
    rhs = jnp.concatenate([ref[...] for ref in refs[n_dp:-1]], axis=0)
    refs[-1][...] = dot(lhs, rhs, ((0,), (0,)))


def pick_body(experts, ids_ref, within_ref, table_ref, out_ref):
    ids = ids_ref[...]
    tokens = ids.shape[1]
    at = jnp.broadcast_to(within_ref[...], (experts, tokens))
    values = jnp.take_along_axis(table_ref[:, 0, :], at, axis=1, mode="promise_in_bounds")
    member = iota((experts, tokens), 0) == ids
    out_ref[...] = jnp.sum(jnp.where(member, values, 0.0), axis=0, keepdims=True)


def shards(n_dp, experts, grad_out, route_prob, expert_ids, saved_act, down_weight):
    slots, ffw = saved_act.shape[2:]
    cap = slots // experts
    tokens, width = grad_out.shape
    chunk = width // n_dp
    stored = saved_act[0, 0]
    order = ORDER if experts == len(ORDER) else ()
    chunks = max(len(order), 1)
    ids = expert_ids.reshape(1, tokens)
    prob_row = route_prob.reshape(1, tokens)

    def swap(array, axis, k):
        size = lax.axis_size(axis)
        return lax.ppermute(array, axis, [(r, r ^ k) for r in range(size)])

    def exchange(array):
        return lax.all_to_all(array, "expert", split_axis=0, concat_axis=0, tiled=True)

    *packed, within = kernel_call(
        functools.partial(place_body, experts, order, cap),
        (shape((slots // chunks, width + LANES), BF16),) * chunks + (shape((1, tokens), jnp.int32),),
        (ids, prob_row, grad_out),
        flops=2 * slots * tokens * width,
        name="place",
        stay=(0, 1, 2),
        scratch=(
            pltpu.VMEM((1, tokens), jnp.int32),
            pltpu.VMEM((1, tokens), BF16),
            pltpu.VMEM((tokens, width), BF16),
            pltpu.SemaphoreType.DMA((3,)),
        ),
    )
    (weight,) = kernel_call(
        fetch_body,
        (shape((ffw, width), BF16),),
        (lax.optimization_barrier((down_weight[0], within))[0],),
        flops=2 * slots * width * ffw,
        name="fetch",
        stay=(0,),
        scratch=(pltpu.SemaphoreType.DMA(()),),
    )
    if order:
        arrived = [swap(rows, "expert", k) if k else rows for k, rows in zip(order, packed)]
    else:
        arrived = [exchange(packed[0])]
    replicas = [*range(2, n_dp), 1, 0]
    late, weight = lax.optimization_barrier((stored, weight))
    all_stored = [
        swap(stored if k == replicas[0] else late, "dp", k) if k else stored for k in replicas
    ]

    rows, prob, *weighted = kernel_call(
        functools.partial(weigh_body, replicas, order),
        (shape((slots, width), BF16), shape((slots, LANES), F32))
        + (shape((slots, chunk), BF16),) * n_dp,
        arrived,
        flops=2 * slots * width,
        name="weigh",
        scratch=(pltpu.VMEM((slots, width + LANES), F32),),
    )
    weighted = [swap(rows, "dp", k) if k else rows for k, rows in zip(replicas, weighted)]
    grad_act, table = kernel_call(
        functools.partial(act_body, experts, cap),
        (shape((slots, ffw), BF16), shape((experts, 8, LANES), F32)),
        (rows, prob, weight, stored),
        flops=2 * slots * width * ffw,
        name="act",
    )
    returned = exchange(table)
    (grad_weight,) = kernel_call(
        functools.partial(gradient_body, n_dp),
        (shape((chunk, ffw), F32),),
        (*weighted, *all_stored),
        flops=2 * n_dp * slots * chunk * ffw,
        name="gradient",
    )
    returned, grad_weight = lax.optimization_barrier((returned, grad_weight))
    (grad_prob,) = kernel_call(
        functools.partial(pick_body, experts),
        (shape((1, tokens), F32),),
        (ids, within, returned),
        name="pick",
    )
    return (grad_act[None, None], grad_weight[None], grad_prob.reshape(tokens, 1))


def solution(mesh):
    return jax.shard_map(
        functools.partial(shards, mesh.shape["dp"], mesh.shape["expert"]),
        mesh=mesh,
        in_specs=(
            P(("dp", "expert"), None),
            P(("dp", "expert"), None),
            P(("dp", "expert"), None),
            P("dp", "expert", None, None),
            P("expert", None, None),
        ),
        out_specs=(
            P("dp", "expert", None, None),
            P("expert", "dp", None),
            P(("dp", "expert"), None),
        ),
        check_vma=False,
    )
```

```python
import functools

import jax
import jax.numpy as jnp
from jax import lax
from jax.experimental import pallas as pl
from jax.experimental.pallas import tpu as pltpu
from jax.sharding import PartitionSpec as P

LANES = 128
F32 = jnp.float32
BF16 = jnp.bfloat16
ORDER = (7, 1, 2, 6, 5, 4, 3, 0)


def kernel_call(body, outs, operands, name, flops=0, scratch=(), stay=()):
    nbytes = sum(a.size * a.dtype.itemsize for a in (*outs, *operands))
    vmem, hbm = pl.BlockSpec(memory_space=pltpu.VMEM), pl.BlockSpec(memory_space=pltpu.HBM)
    operands = [
        pltpu.with_memory_space_constraint(a, pltpu.HBM) if i in stay else a
        for i, a in enumerate(operands)
    ]
    return pl.pallas_call(
        body,
        out_shape=outs,
        in_specs=[hbm if i in stay else vmem for i in range(len(operands))],
        out_specs=[vmem] * len(outs),
        scratch_shapes=scratch,
        compiler_params=pltpu.CompilerParams(vmem_limit_bytes=16 * 2**20),
        cost_estimate=pl.CostEstimate(flops=flops, bytes_accessed=nbytes, transcendentals=0),
        name=name,
    )(*operands)


def shape(dims, kind):
    return jax.ShapeDtypeStruct(dims, kind)


def dot(a, b, dims=((1,), (0,)), precision=None):
    return lax.dot_general(
        a, b, (dims, ((), ())), preferred_element_type=F32, precision=precision
    )


def iota(dims, axis):
    return lax.broadcasted_iota(jnp.int32, dims, axis)


def place_body(experts, order, cap, *refs):
    (ids_hbm, prob_hbm, rows_hbm), refs = refs[:3], refs[3:]
    *chunk_refs, within_ref, ids_ref, prob_ref, rows_ref, sems = refs
    copies = [
        pltpu.make_async_copy(source, target, sems.at[i])
        for i, (source, target) in enumerate(
            ((ids_hbm, ids_ref), (prob_hbm, prob_ref), (rows_hbm, rows_ref))
        )
    ]
    for copy in copies:
        copy.start()
    tokens, width = rows_ref.shape
    copies[0].wait()
    ids = ids_ref[...]
    slots, rows = experts * cap, chunk_refs[0].shape[0]
    member = (iota((experts, tokens), 0) == ids).astype(F32)
    earlier = (iota((tokens, tokens), 0) < iota((tokens, tokens), 1)).astype(BF16)
    before = dot(member.astype(BF16), earlier)
    within = jnp.sum(before * member, axis=0, keepdims=True).astype(jnp.int32)
    within_ref[...] = within
    partner = ids ^ lax.axis_index("expert")
    place = 0
    for i, k in enumerate(order):
        place = jnp.where(partner == k, i, place)
    if not order:
        place = ids
    chosen = iota((slots, tokens), 0) == place * cap + within
    copies[1].wait()
    prob = jnp.sum(jnp.where(chosen, prob_ref[...].astype(F32), 0.0), axis=1, keepdims=True)
    chosen = chosen.astype(BF16)
    copies[2].wait()

    def put(columns, values):
        for i, ref in enumerate(chunk_refs):
            ref[:, columns] = values[i * rows : (i + 1) * rows].astype(BF16)

    step = 2 * LANES
    for c in range(0, width, step):
        put(slice(c, c + step), dot(chosen, rows_ref[:, c : c + step]))
    put(slice(width, width + LANES), jnp.broadcast_to(prob, (slots, LANES)))


def weigh_body(replicas, order, *refs):
    n_dp = len(replicas)
    *chunk_refs, rows_ref, prob_ref = refs[: -n_dp - 1]
    weighted_refs, all_ref = refs[-n_dp - 1 : -1], refs[-1]
    width = rows_ref.shape[1]
    chunk = width // n_dp
    size = chunk_refs[0].shape[0]
    for c in range(0, width + LANES, LANES):
        columns = slice(c, c + LANES)
        for k, ref in zip(order or (0,), chunk_refs):
            at = (lax.axis_index("expert") ^ k) * size if order else 0
            all_ref[pl.ds(at, size), columns] = ref[:, columns].astype(F32)
    prob = all_ref[:, width:]
    prob_ref[...] = prob
    replica = lax.axis_index("dp")
    for k, ref in zip(replicas, weighted_refs):
        for c in range(0, chunk, LANES):
            columns = pl.ds(pl.multiple_of((replica ^ k) * chunk + c, LANES), LANES)
            piece = all_ref[:, columns]
            rows_ref[:, columns] = piece.astype(BF16)
            ref[:, c : c + LANES] = (piece * prob).astype(BF16)


def fetch_body(weight_hbm, out_ref, sem):
    copy = pltpu.make_async_copy(weight_hbm, out_ref, sem)
    copy.start()
    copy.wait()


def by_source(column, experts, cap):
    slots = experts * cap
    spread = jnp.where(iota((slots, LANES), 1) == iota((slots, LANES), 0) % cap, column, 0.0)
    if cap % 8 == 0:
        return jnp.sum(spread.reshape(experts, cap, LANES), axis=1)
    owner = (iota((experts, slots), 0) == iota((experts, slots), 1) // cap).astype(F32)
    return dot(owner, spread, precision=lax.Precision.HIGHEST)


def act_body(experts, cap, rows_ref, prob_ref, weight_ref, stored_ref, act_ref, table_ref):
    backed = dot(rows_ref[...], weight_ref[...], ((1,), (1,)))
    act_ref[...] = (prob_ref[:, 0:1] * backed).astype(BF16)
    column = jnp.sum(backed * stored_ref[...].astype(F32), axis=1, keepdims=True)
    table = by_source(column, experts, cap)
    table_ref[...] = jnp.broadcast_to(table[:, None], table_ref.shape)


def gradient_body(n_dp, *refs):
    lhs = jnp.concatenate([ref[...] for ref in refs[:n_dp]], axis=0)
    rhs = jnp.concatenate([ref[...] for ref in refs[n_dp:-1]], axis=0)
    refs[-1][...] = dot(lhs, rhs, ((0,), (0,)))


def pick_body(experts, ids_ref, within_ref, table_ref, out_ref):
    ids = ids_ref[...]
    tokens = ids.shape[1]
    at = jnp.broadcast_to(within_ref[...], (experts, tokens))
    values = jnp.take_along_axis(table_ref[:, 0, :], at, axis=1, mode="promise_in_bounds")
    member = iota((experts, tokens), 0) == ids
    out_ref[...] = jnp.sum(jnp.where(member, values, 0.0), axis=0, keepdims=True)


def shards(n_dp, experts, grad_out, route_prob, expert_ids, saved_act, down_weight):
    slots, ffw = saved_act.shape[2:]
    cap = slots // experts
    tokens, width = grad_out.shape
    chunk = width // n_dp
    stored = saved_act[0, 0]
    order = ORDER if experts == len(ORDER) else ()
    chunks = max(len(order), 1)
    ids = expert_ids.reshape(1, tokens)
    prob_row = route_prob.reshape(1, tokens)

    def swap(array, axis, k):
        size = lax.axis_size(axis)
        return lax.ppermute(array, axis, [(r, r ^ k) for r in range(size)])

    def exchange(array):
        return lax.all_to_all(array, "expert", split_axis=0, concat_axis=0, tiled=True)

    *packed, within = kernel_call(
        functools.partial(place_body, experts, order, cap),
        (shape((slots // chunks, width + LANES), BF16),) * chunks + (shape((1, tokens), jnp.int32),),
        (ids, prob_row, grad_out),
        flops=2 * slots * tokens * width,
        name="place",
        stay=(0, 1, 2),
        scratch=(
            pltpu.VMEM((1, tokens), jnp.int32),
            pltpu.VMEM((1, tokens), BF16),
            pltpu.VMEM((tokens, width), BF16),
            pltpu.SemaphoreType.DMA((3,)),
        ),
    )
    (weight,) = kernel_call(
        fetch_body,
        (shape((ffw, width), BF16),),
        (lax.optimization_barrier((down_weight[0], within))[0],),
        flops=2 * slots * width * ffw,
        name="fetch",
        stay=(0,),
        scratch=(pltpu.SemaphoreType.DMA(()),),
    )
    if order:
        arrived = [swap(rows, "expert", k) if k else rows for k, rows in zip(order, packed)]
    else:
        arrived = [exchange(packed[0])]
    replicas = [*range(2, n_dp), 1, 0]
    late, weight = lax.optimization_barrier((stored, weight))
    all_stored = [
        swap(stored if k == replicas[0] else late, "dp", k) if k else stored for k in replicas
    ]

    rows, prob, *weighted = kernel_call(
        functools.partial(weigh_body, replicas, order),
        (shape((slots, width), BF16), shape((slots, LANES), F32))
        + (shape((slots, chunk), BF16),) * n_dp,
        arrived,
        flops=2 * slots * width,
        name="weigh",
        scratch=(pltpu.VMEM((slots, width + LANES), F32),),
    )
    weighted = [swap(rows, "dp", k) if k else rows for k, rows in zip(replicas, weighted)]
    grad_act, table = kernel_call(
        functools.partial(act_body, experts, cap),
        (shape((slots, ffw), BF16), shape((experts, 8, LANES), F32)),
        (rows, prob, weight, stored),
        flops=2 * slots * width * ffw,
        name="act",
    )
    returned = exchange(table)
    (grad_weight,) = kernel_call(
        functools.partial(gradient_body, n_dp),
        (shape((chunk, ffw), F32),),
        (*weighted, *all_stored),
        flops=2 * n_dp * slots * chunk * ffw,
        name="gradient",
    )
    returned, grad_weight = lax.optimization_barrier((returned, grad_weight))
    (grad_prob,) = kernel_call(
        functools.partial(pick_body, experts),
        (shape((1, tokens), F32),),
        (ids, within, returned),
        name="pick",
    )
    return (grad_act[None, None], grad_weight[None], grad_prob.reshape(tokens, 1))


def solution(mesh):
    return jax.shard_map(
        functools.partial(shards, mesh.shape["dp"], mesh.shape["expert"]),
        mesh=mesh,
        in_specs=(
            P(("dp", "expert"), None),
            P(("dp", "expert"), None),
            P(("dp", "expert"), None),
            P("dp", "expert", None, None),
            P("expert", None, None),
        ),
        out_specs=(
            P("dp", "expert", None, None),
            P("expert", "dp", None),
            P(("dp", "expert"), None),
        ),
        check_vma=False,
    )
```

```python
import functools

import jax
import jax.numpy as jnp
from jax import lax
from jax.experimental import pallas as pl
from jax.experimental.pallas import tpu as pltpu
from jax.sharding import PartitionSpec as P

LANES = 128
F32 = jnp.float32
BF16 = jnp.bfloat16
ORDER = (6, 2, 1, 7, 5, 4, 3, 0)


def kernel_call(body, outs, operands, name, flops=0, scratch=(), stay=()):
    nbytes = sum(a.size * a.dtype.itemsize for a in (*outs, *operands))
    vmem, hbm = pl.BlockSpec(memory_space=pltpu.VMEM), pl.BlockSpec(memory_space=pltpu.HBM)
    operands = [
        pltpu.with_memory_space_constraint(a, pltpu.HBM) if i in stay else a
        for i, a in enumerate(operands)
    ]
    return pl.pallas_call(
        body,
        out_shape=outs,
        in_specs=[hbm if i in stay else vmem for i in range(len(operands))],
        out_specs=[vmem] * len(outs),
        scratch_shapes=scratch,
        compiler_params=pltpu.CompilerParams(vmem_limit_bytes=16 * 2**20),
        cost_estimate=pl.CostEstimate(flops=flops, bytes_accessed=nbytes, transcendentals=0),
        name=name,
    )(*operands)


def shape(dims, kind):
    return jax.ShapeDtypeStruct(dims, kind)


def dot(a, b, dims=((1,), (0,)), precision=None):
    return lax.dot_general(
        a, b, (dims, ((), ())), preferred_element_type=F32, precision=precision
    )


def iota(dims, axis):
    return lax.broadcasted_iota(jnp.int32, dims, axis)


def place_body(experts, order, cap, *refs):
    (ids_hbm, prob_hbm, rows_hbm), refs = refs[:3], refs[3:]
    *chunk_refs, within_ref, ids_ref, prob_ref, rows_ref, sems = refs
    copies = [
        pltpu.make_async_copy(source, target, sems.at[i])
        for i, (source, target) in enumerate(
            ((ids_hbm, ids_ref), (prob_hbm, prob_ref), (rows_hbm, rows_ref))
        )
    ]
    for copy in copies:
        copy.start()
    tokens, width = rows_ref.shape
    copies[0].wait()
    ids = ids_ref[...]
    slots, rows = experts * cap, chunk_refs[0].shape[0]
    member = (iota((experts, tokens), 0) == ids).astype(F32)
    earlier = (iota((tokens, tokens), 0) < iota((tokens, tokens), 1)).astype(BF16)
    before = dot(member.astype(BF16), earlier)
    within = jnp.sum(before * member, axis=0, keepdims=True).astype(jnp.int32)
    within_ref[...] = within
    partner = ids ^ lax.axis_index("expert")
    place = 0
    for i, k in enumerate(order):
        place = jnp.where(partner == k, i, place)
    if not order:
        place = ids
    chosen = iota((slots, tokens), 0) == place * cap + within
    copies[1].wait()
    prob = jnp.sum(jnp.where(chosen, prob_ref[...].astype(F32), 0.0), axis=1, keepdims=True)
    chosen = chosen.astype(BF16)
    copies[2].wait()

    def put(columns, values):
        for i, ref in enumerate(chunk_refs):
            ref[:, columns] = values[i * rows : (i + 1) * rows].astype(BF16)

    step = 2 * LANES
    for c in range(0, width, step):
        put(slice(c, c + step), dot(chosen, rows_ref[:, c : c + step]))
    put(slice(width, width + LANES), jnp.broadcast_to(prob, (slots, LANES)))


def weigh_body(replicas, order, *refs):
    n_dp = len(replicas)
    *chunk_refs, rows_ref, prob_ref = refs[: -n_dp - 1]
    weighted_refs, all_ref = refs[-n_dp - 1 : -1], refs[-1]
    width = rows_ref.shape[1]
    chunk = width // n_dp
    size = chunk_refs[0].shape[0]
    for c in range(0, width + LANES, LANES):
        columns = slice(c, c + LANES)
        for k, ref in zip(order or (0,), chunk_refs):
            at = (lax.axis_index("expert") ^ k) * size if order else 0
            all_ref[pl.ds(at, size), columns] = ref[:, columns].astype(F32)
    prob = all_ref[:, width:]
    prob_ref[...] = prob
    replica = lax.axis_index("dp")
    for k, ref in zip(replicas, weighted_refs):
        for c in range(0, chunk, LANES):
            columns = pl.ds(pl.multiple_of((replica ^ k) * chunk + c, LANES), LANES)
            piece = all_ref[:, columns]
            rows_ref[:, columns] = piece.astype(BF16)
            ref[:, c : c + LANES] = (piece * prob).astype(BF16)


def fetch_body(weight_hbm, out_ref, sem):
    copy = pltpu.make_async_copy(weight_hbm, out_ref, sem)
    copy.start()
    copy.wait()


def by_source(column, experts, cap):
    slots = experts * cap
    spread = jnp.where(iota((slots, LANES), 1) == iota((slots, LANES), 0) % cap, column, 0.0)
    if cap % 8 == 0:
        return jnp.sum(spread.reshape(experts, cap, LANES), axis=1)
    owner = (iota((experts, slots), 0) == iota((experts, slots), 1) // cap).astype(F32)
    return dot(owner, spread, precision=lax.Precision.HIGHEST)


def act_body(experts, cap, rows_ref, prob_ref, weight_ref, stored_ref, act_ref, table_ref):
    backed = dot(rows_ref[...], weight_ref[...], ((1,), (1,)))
    act_ref[...] = (prob_ref[:, 0:1] * backed).astype(BF16)
    column = jnp.sum(backed * stored_ref[...].astype(F32), axis=1, keepdims=True)
    table = by_source(column, experts, cap)
    table_ref[...] = jnp.broadcast_to(table[:, None], table_ref.shape)


def gradient_body(n_dp, *refs):
    lhs = jnp.concatenate([ref[...] for ref in refs[:n_dp]], axis=0)
    rhs = jnp.concatenate([ref[...] for ref in refs[n_dp:-1]], axis=0)
    refs[-1][...] = dot(lhs, rhs, ((0,), (0,)))


def pick_body(experts, ids_ref, within_ref, table_ref, out_ref):
    ids = ids_ref[...]
    tokens = ids.shape[1]
    at = jnp.broadcast_to(within_ref[...], (experts, tokens))
    values = jnp.take_along_axis(table_ref[:, 0, :], at, axis=1, mode="promise_in_bounds")
    member = iota((experts, tokens), 0) == ids
    out_ref[...] = jnp.sum(jnp.where(member, values, 0.0), axis=0, keepdims=True)


def shards(n_dp, experts, grad_out, route_prob, expert_ids, saved_act, down_weight):
    slots, ffw = saved_act.shape[2:]
    cap = slots // experts
    tokens, width = grad_out.shape
    chunk = width // n_dp
    stored = saved_act[0, 0]
    order = ORDER if experts == len(ORDER) else ()
    chunks = max(len(order), 1)
    ids = expert_ids.reshape(1, tokens)
    prob_row = route_prob.reshape(1, tokens)

    def swap(array, axis, k):
        size = lax.axis_size(axis)
        return lax.ppermute(array, axis, [(r, r ^ k) for r in range(size)])

    def exchange(array):
        return lax.all_to_all(array, "expert", split_axis=0, concat_axis=0, tiled=True)

    *packed, within = kernel_call(
        functools.partial(place_body, experts, order, cap),
        (shape((slots // chunks, width + LANES), BF16),) * chunks + (shape((1, tokens), jnp.int32),),
        (ids, prob_row, grad_out),
        flops=2 * slots * tokens * width,
        name="place",
        stay=(0, 1, 2),
        scratch=(
            pltpu.VMEM((1, tokens), jnp.int32),
            pltpu.VMEM((1, tokens), BF16),
            pltpu.VMEM((tokens, width), BF16),
            pltpu.SemaphoreType.DMA((3,)),
        ),
    )
    (weight,) = kernel_call(
        fetch_body,
        (shape((ffw, width), BF16),),
        (lax.optimization_barrier((down_weight[0], within))[0],),
        flops=2 * slots * width * ffw,
        name="fetch",
        stay=(0,),
        scratch=(pltpu.SemaphoreType.DMA(()),),
    )
    if order:
        arrived = [swap(rows, "expert", k) if k else rows for k, rows in zip(order, packed)]
    else:
        arrived = [exchange(packed[0])]
    replicas = [*range(2, n_dp), 1, 0]
    late, weight = lax.optimization_barrier((stored, weight))
    all_stored = [
        swap(stored if k == replicas[0] else late, "dp", k) if k else stored for k in replicas
    ]

    rows, prob, *weighted = kernel_call(
        functools.partial(weigh_body, replicas, order),
        (shape((slots, width), BF16), shape((slots, LANES), F32))
        + (shape((slots, chunk), BF16),) * n_dp,
        arrived,
        flops=2 * slots * width,
        name="weigh",
        scratch=(pltpu.VMEM((slots, width + LANES), F32),),
    )
    weighted = [swap(rows, "dp", k) if k else rows for k, rows in zip(replicas, weighted)]
    grad_act, table = kernel_call(
        functools.partial(act_body, experts, cap),
        (shape((slots, ffw), BF16), shape((experts, 8, LANES), F32)),
        (rows, prob, weight, stored),
        flops=2 * slots * width * ffw,
        name="act",
    )
    returned = exchange(table)
    (grad_weight,) = kernel_call(
        functools.partial(gradient_body, n_dp),
        (shape((chunk, ffw), F32),),
        (*weighted, *all_stored),
        flops=2 * n_dp * slots * chunk * ffw,
        name="gradient",
    )
    returned, grad_weight = lax.optimization_barrier((returned, grad_weight))
    (grad_prob,) = kernel_call(
        functools.partial(pick_body, experts),
        (shape((1, tokens), F32),),
        (ids, within, returned),
        name="pick",
    )
    return (grad_act[None, None], grad_weight[None], grad_prob.reshape(tokens, 1))


def solution(mesh):
    return jax.shard_map(
        functools.partial(shards, mesh.shape["dp"], mesh.shape["expert"]),
        mesh=mesh,
        in_specs=(
            P(("dp", "expert"), None),
            P(("dp", "expert"), None),
            P(("dp", "expert"), None),
            P("dp", "expert", None, None),
            P("expert", None, None),
        ),
        out_specs=(
            P("dp", "expert", None, None),
            P("expert", "dp", None),
            P(("dp", "expert"), None),
        ),
        check_vma=False,
    )
```
